256 devices in a mesh: grp: 64 (over z_lo, y, x), tp: 4 (over z_hi, core).
Axes of the slice: x: 4, y: 4, z: 8 (z_hi: 2, z_lo: 4; z = z_hi * 4 + z_lo), core: 2. Of those that a mesh axis runs over, the one named last changes fastest.
Arguments:
- comp_queries: bfloat16 [16384, 8192], P('grp', 'tp'), may hold values from -6 to 6
- comp_keys: bfloat16 [16384, 1024], P('grp', 'tp'), may hold values from -6 to 6
- comp_values: bfloat16 [16384, 1024], P('grp', 'tp'), may hold values from -6 to 6
- prompt_keys: bfloat16 [768, 1024], P('grp', 'tp'), may hold values from -6 to 6
- prompt_values: bfloat16 [768, 1024], P('grp', 'tp'), may hold values from -6 to 6
- query_gain: float32 [128], replicated, may hold values from 0.5 to 6
- key_gain: float32 [128], replicated, may hold values from 0.5 to 6
- out_grad: bfloat16 [16384, 8192], P('grp', 'tp'), may hold values from -18 to 18
- live_counts: int32 [64], P('grp'), may hold values from 1 to 4, as said below
- slot_prompts: int32 [256], P('grp'), may hold values from 0 to 1, as said below
Outputs:
- attended: bfloat16 [16384, 8192], P('grp', 'tp')
- query_grads: bfloat16 [16384, 8192], P('grp', 'tp')
- comp_key_grads: bfloat16 [16384, 1024], P('grp', 'tp')
- comp_value_grads: bfloat16 [16384, 1024], P('grp', 'tp')
- prompt_key_grads: float32 [768, 1024], P('grp', 'tp')
- prompt_value_grads: float32 [768, 1024], P('grp', 'tp')
- query_gain_grad: float32 [128], replicated
- key_gain_grad: float32 [128], replicated
The draws below stay inside these ranges and needn't reach their ends.
Inputs may be any that keep to these rules, and one draw needn't show every extreme that they name: Slot j of index s of grp is live exactly when j < live_counts[s]; some index has all 4 live and some has one. `slot_prompts`: the first slot of every index of grp is live; every prompt is named by some first slot.
All inputs are finite; a program needn't handle non-finite values.
Results may differ from the reference program's by a relative error of at most 0.033.
The reference program's roundings to bfloat16 on the way count: a program that leaves them out, or rounds other values in their place, can miss the bound.
Values may be sent and summed in bfloat16 or wider, within the bound.
A program may use at most 64 MiB of HBM per device.

```python
import math
import jax
import jax.numpy as jnp
from jax import lax

H = 64
KVH = 8
HD = 128
PL = 384
CL = 64
SLOTS = 4
COMP_DEVS = 64
PROMPTS = 2
COMPLETIONS = 256
CTOKENS = 16384
POOL = 768


def draw_comp_queries(key, part):
    key = jax.random.fold_in(key, 11)
    return jnp.clip(jax.random.normal(key, (CTOKENS, H * HD), jnp.float32), -6.0, 6.0).astype(jnp.bfloat16)


def draw_prompt_keys(key, part):
    key = jax.random.fold_in(key, 13)
    return jnp.clip(jax.random.normal(key, (POOL, KVH * HD), jnp.float32), -6.0, 6.0).astype(jnp.bfloat16)


def gain_draw(key):
    return jnp.exp(jax.random.uniform(key, (HD,), jnp.float32, -0.69, 0.69))


def draw_query_gain(key, part):
    key = jax.random.fold_in(key, 17)
    return gain_draw(key)


def draw_key_gain(key, part):
    key = jax.random.fold_in(key, 19)
    return gain_draw(key)


def draw_out_grad(key, part):
    key = jax.random.fold_in(key, 23)
    rising = jnp.arange(CTOKENS).astype(jnp.float32) / CTOKENS
    noise_part = jnp.clip(jax.random.normal(key, (CTOKENS, H * HD), jnp.float32), -6.0, 6.0)
    return (noise_part * (1.0 + 2.0 * rising)[:, None]).astype(jnp.bfloat16)


def draw_live_counts(key, part):
    key = jax.random.fold_in(key, 29)
    subkeys = jax.random.split(key, 3)
    values = jax.random.randint(subkeys[0], (COMP_DEVS,), 1, SLOTS + 1)
    busiest = jax.random.randint(subkeys[1], (), 0, COMP_DEVS)
    lightest = (busiest + jax.random.randint(subkeys[2], (), 1, COMP_DEVS)) % COMP_DEVS
    position = jnp.arange(COMP_DEVS)
    values = jnp.where(position == busiest, SLOTS, values)
    return jnp.where(position == lightest, 1, values).astype(jnp.int32)


def draw_slot_prompts(key, part):
    key = jax.random.fold_in(key, 31)
    subkeys = jax.random.split(key, 2)
    shuffled = jax.random.permutation(subkeys[0], COMP_DEVS) % PROMPTS
    others = jax.random.randint(subkeys[1], (COMP_DEVS, SLOTS), 0, PROMPTS)
    column = jnp.arange(SLOTS)[None, :]
    return jnp.where(column == 0, shuffled[:, None], others).reshape(COMPLETIONS).astype(jnp.int32)


def levels(stream_key, shape, shards, least, largest):
    loudness, own = 1.0, jax.random.fold_in(stream_key, 6)
    for axis_at, shards_of in shards:
        heights = jnp.exp(jax.random.uniform(jax.random.fold_in(own, axis_at), (shards_of,), jnp.float32, least / len(shards), largest / len(shards)))
        loudness = loudness * jnp.repeat(heights, shape[axis_at] // shards_of).reshape([-1 if axis == axis_at else 1 for axis in range(len(shape))])
    return loudness


def gaussian(own_key, shape, width, limit, cuts=(), held_as=jnp.bfloat16):
    entries = jax.random.normal(own_key, shape, jnp.float32) * width
    if len(cuts) > 0:
        entries = levels(own_key, shape, cuts, -0.22, 0.18) * entries
    return jnp.clip(entries, min=-limit, max=limit).astype(held_as)


def setup_inputs(seed: int = 0) -> dict:
    key_of = jax.random.split(jax.random.key(seed), 11)
    return {
        "comp_queries": draw_comp_queries(jax.random.fold_in(key_of[10], 71), 0),
        "comp_keys": gaussian(key_of[1], (CTOKENS, KVH * HD), 1.0, 6.0, ((0, 64), (1, 4))),
        "comp_values": gaussian(key_of[2], (CTOKENS, KVH * HD), 1.0, 6.0, ((0, 64), (1, 4))),
        "prompt_keys": draw_prompt_keys(jax.random.fold_in(key_of[10], 71), 0),
        "prompt_values": gaussian(key_of[4], (POOL, KVH * HD), 1.0, 6.0, ((0, 64), (1, 4))),
        "query_gain": draw_query_gain(jax.random.fold_in(key_of[10], 71), 0),
        "key_gain": draw_key_gain(jax.random.fold_in(key_of[10], 71), 0),
        "out_grad": draw_out_grad(jax.random.fold_in(key_of[10], 71), 0),
        "live_counts": draw_live_counts(jax.random.fold_in(key_of[10], 71), 0),
        "slot_prompts": draw_slot_prompts(jax.random.fold_in(key_of[10], 71), 0),
    }


epsilon = 1e-06

def normalize(raw_rows, gain_row):
    values = raw_rows.astype(jnp.float32)
    reciprocal = lax.rsqrt(lax.optimization_barrier(jnp.mean(values * values, axis=-1, keepdims=True)) + epsilon)
    unit_rows = values * reciprocal
    return (unit_rows * gain_row, unit_rows, reciprocal)

def norm_back(upstream, unit_rows, reciprocal, gain_row):
    scaled = upstream * gain_row
    return reciprocal * (scaled - unit_rows * lax.optimization_barrier(jnp.mean(unit_rows * scaled, axis=-1, keepdims=True)))

def product(form, left, right):
    return jnp.einsum(form, left.astype(jnp.float32), right.astype(jnp.float32), precision=lax.Precision.HIGHEST)

def to_half(values):
    return lax.optimization_barrier(values.astype(jnp.bfloat16)).astype(jnp.float32)

def block_scores(queries, key_block):
    score_scale = 1.0 / math.sqrt(queries.shape[-1])
    return product('qkgd,nkd->kgqn', queries, key_block) * score_scale

def back_block(queries, grads_out, log_total, row_delta, key_block, value_block, allowed):
    score_scale = 1.0 / math.sqrt(queries.shape[-1])
    scores = block_scores(queries, key_block)
    probability = jnp.where(allowed, jnp.exp(scores - log_total[..., None]), 0.0)
    value_grad = product('kgqn,qkgd->nkd', to_half(probability), grads_out)
    prob_grad = product('qkgd,nkd->kgqn', grads_out, value_block)
    score_grad = to_half(probability * (prob_grad - row_delta[..., None]))
    query_grad = product('kgqn,nkd->qkgd', score_grad, key_block) * score_scale
    key_grad = product('kgqn,qkgd->nkd', score_grad, queries) * score_scale
    return (query_grad, key_grad, value_grad)

def reference(comp_queries, comp_keys, comp_values, prompt_keys, prompt_values, query_gain, key_gain, out_grad, live_counts, slot_prompts):
    group_size = H // KVH
    prompt_norm, prompt_unit, prompt_recip = normalize(prompt_keys.reshape(POOL, KVH, HD), key_gain)
    prompt_half = prompt_norm.astype(jnp.bfloat16)
    prompt_value_rows = prompt_values.reshape(POOL, KVH, HD)
    live_mask = jnp.arange(COMPLETIONS) % SLOTS < jnp.repeat(live_counts, SLOTS, total_repeat_length=COMPLETIONS)
    causal = jnp.arange(CL)[:, None] >= jnp.arange(CL)[None, :]
    allowed = jnp.concatenate([jnp.ones((CL, PL), bool), causal], axis=1)

    def scan_step(carried, scan_item):
        pool_key_grad, pool_value_grad, query_part, key_part = carried
        raw_queries, raw_keys, own_values, grads_out, prompt_no, alive = scan_item
        query_norm, query_unit, query_recip = normalize(raw_queries, query_gain)
        queries = query_norm.astype(jnp.bfloat16)
        key_norm, key_unit, key_recip = normalize(raw_keys, key_gain)
        own_keys = key_norm.astype(jnp.bfloat16)
        first_row = (prompt_no * PL).astype(jnp.int32)
        key_block = jnp.concatenate([lax.dynamic_slice_in_dim(prompt_half, first_row, PL, 0), own_keys], axis=0)
        value_block = jnp.concatenate([lax.dynamic_slice_in_dim(prompt_value_rows, first_row, PL, 0), own_values], axis=0)
        scores = jnp.where(allowed, block_scores(queries, key_block), -jnp.inf)
        row_high = lax.optimization_barrier(jnp.max(scores, axis=-1))
        weights = jnp.exp(scores - row_high[..., None])
        sum_total = lax.optimization_barrier(jnp.sum(weights, axis=-1))
        attended_rows = product('kgqn,nkd->kgqd', weights, value_block) / sum_total[..., None]
        log_total = row_high + jnp.log(sum_total)
        out_half = jnp.where(alive, jnp.transpose(attended_rows, (2, 0, 1, 3)), 0.0).astype(jnp.bfloat16)
        row_delta = jnp.transpose(lax.optimization_barrier(jnp.sum(grads_out.astype(jnp.float32) * out_half.astype(jnp.float32), axis=-1)), (1, 2, 0))
        query_grad, key_grad, value_grad = back_block(queries, grads_out, log_total, row_delta, key_block, value_block, allowed)
        query_grad = jnp.where(alive, query_grad, 0.0)
        key_grad = jnp.where(alive, key_grad, 0.0)
        value_grad = jnp.where(alive, value_grad, 0.0)
        prior_keys = lax.dynamic_slice_in_dim(pool_key_grad, first_row, PL, 0)
        pool_key_grad = lax.dynamic_update_slice_in_dim(pool_key_grad, prior_keys + key_grad[:PL], first_row, 0)
        prior_values = lax.dynamic_slice_in_dim(pool_value_grad, first_row, PL, 0)
        pool_value_grad = lax.dynamic_update_slice_in_dim(pool_value_grad, prior_values + value_grad[:PL], first_row, 0)
        query_part = query_part + lax.optimization_barrier(jnp.sum(query_grad * query_unit, axis=(0, 1, 2)))
        key_part = key_part + lax.optimization_barrier(jnp.sum(key_grad[PL:] * key_unit, axis=(0, 1)))
        query_out = norm_back(query_grad, query_unit, query_recip, query_gain).astype(jnp.bfloat16)
        key_out = norm_back(key_grad[PL:], key_unit, key_recip, key_gain).astype(jnp.bfloat16)
        value_out = value_grad[PL:].astype(jnp.bfloat16)
        return ((pool_key_grad, pool_value_grad, query_part, key_part), (out_half, query_out, key_out, value_out))
    start = (jnp.zeros((POOL, KVH, HD), jnp.float32), jnp.zeros((POOL, KVH, HD), jnp.float32), jnp.zeros((HD,), jnp.float32), jnp.zeros((HD,), jnp.float32))
    scan_items = (comp_queries.reshape(COMPLETIONS, CL, KVH, group_size, HD), comp_keys.reshape(COMPLETIONS, CL, KVH, HD), comp_values.reshape(COMPLETIONS, CL, KVH, HD), out_grad.reshape(COMPLETIONS, CL, KVH, group_size, HD), slot_prompts, live_mask)
    finals, stacked = lax.scan(scan_step, start, scan_items)
    pool_key_grad, pool_value_grad, query_part, key_part = finals
    out_half, query_out, key_out, value_out = stacked
    key_part = key_part + lax.optimization_barrier(jnp.sum(pool_key_grad * prompt_unit, axis=(0, 1)))
    prompt_key_grads = norm_back(pool_key_grad, prompt_unit, prompt_recip, key_gain).reshape(POOL, KVH * HD)
    prompt_value_grads = pool_value_grad.reshape(POOL, KVH * HD)
    return (out_half.reshape(CTOKENS, H * HD), query_out.reshape(CTOKENS, H * HD), key_out.reshape(CTOKENS, KVH * HD), value_out.reshape(CTOKENS, KVH * HD), prompt_key_grads, prompt_value_grads, query_part, key_part)
```

```python
import functools
import math

import jax
import jax.numpy as jnp
from jax import lax
from jax.experimental import pallas as pl
from jax.experimental.pallas import tpu as pltpu
from jax.sharding import PartitionSpec as P

HD = 128
CL = 64
PL = 384
HEADS = 8
OWN = 12
PAD = 16
BLOCK = 48
EPS = 1e-6
SCALE = 1.0 / math.sqrt(HD)
EXPONENT = SCALE * math.log2(math.e)
F32 = jnp.float32
BF16 = jnp.bfloat16
MESH = pl.DeviceIdType.MESH


def place():
    grp = lax.axis_index("grp")
    return grp // 16, (grp // 4) % 4, grp % 4, lax.axis_index("tp")


def greet(targets):
    barrier = pltpu.get_barrier_semaphore()
    for target in targets:
        pl.semaphore_signal(barrier, inc=1, device_id=target, device_id_type=MESH)
    pl.semaphore_wait(barrier, len(targets))


def send(source, target_ref, send_sem, recv_sem, target):
    copy = pltpu.make_async_remote_copy(
        src_ref=source,
        dst_ref=target_ref,
        send_sem=send_sem,
        recv_sem=recv_sem,
        device_id=target,
        device_id_type=MESH,
    )
    copy.start()
    return copy


def gather_kernel(
    keys_ref, values_ref, a_ref, b_ref, columns, z_send, z_recv, first_send, first_recv, next_send, next_recv
):
    z, y, x, tp = place()

    def at(zz, yy, xx):
        return (zz * 16 + yy * 4 + xx, tp)

    z_peers = [at((z + d) % 4, y, x) for d in (1, 2, 3)]
    y_peers = [at(z, (y + d) % 4, x) for d in (1, 2, 3)]
    x_peers = [at(z, y, (x + d) % 4) for d in (1, 2, 3)]
    greet(z_peers + y_peers + x_peers)
    mine = jnp.concatenate([keys_ref[...], values_ref[...]], axis=1).astype(F32)
    mine = jnp.concatenate([mine, jnp.zeros((PAD - OWN, 4 * HD), F32)], axis=0)
    columns[z] = mine.astype(BF16)
    copies = [
        send(columns.at[z], columns.at[z], z_send.at[d], z_recv.at[d], z_peers[d]) for d in range(3)
    ]
    for copy in copies:
        copy.wait_recv()
    block = jnp.concatenate([columns[zz].astype(F32)[:OWN] for zz in range(4)], axis=0).astype(BF16)
    a_ref[y, x] = block[:, : 2 * HD]
    b_ref[x, y] = block[:, 2 * HD :]
    halves = ((a_ref, y, x, x_peers, y_peers), (b_ref, x, y, y_peers, x_peers))
    firsts = []
    for half, (ref, slow, fast, near, far) in enumerate(halves):
        firsts.append(
            [
                send(
                    ref.at[slow, fast],
                    ref.at[slow, fast],
                    first_send.at[half, d],
                    first_recv.at[half, d],
                    near[d],
                )
                for d in range(3)
            ]
        )
    later = []
    for back in range(4):
        for half, (ref, slow, fast, near, far) in enumerate(halves):
            if back > 0:
                firsts[half][back - 1].wait_recv()
            held = ref.at[slow, (fast + 4 - back) % 4]
            for d in range(3):
                later.append(
                    send(
                        held, held, next_send.at[half, back, d], next_recv.at[half, back, d], far[d]
                    )
                )
    for copy in later:
        copy.wait_recv()
    for copy in copies + firsts[0] + firsts[1] + later:
        copy.wait_send()


def gather(keys, values):
    shape = jax.ShapeDtypeStruct((4, 4, BLOCK, 2 * HD), BF16)
    vmem = pl.BlockSpec(memory_space=pltpu.VMEM)
    dma = pltpu.SemaphoreType.DMA
    return pl.pallas_call(
        gather_kernel,
        out_shape=[shape, shape],
        in_specs=[vmem, vmem],
        out_specs=[vmem, vmem],
        scratch_shapes=[
            pltpu.VMEM((4, PAD, 4 * HD), BF16),
            dma((3,)),
            dma((3,)),
            dma((2, 3)),
            dma((2, 3)),
            dma((2, 4, 3)),
            dma((2, 4, 3)),
        ],
        compiler_params=pltpu.CompilerParams(collective_id=0, has_side_effects=True),
    )(keys, values)


def dot(left, right, over_left, over_right):
    return lax.dot_general(
        left, right, (((over_left,), (over_right,)), ((), ())), preferred_element_type=F32
    )


def to_rows(block):
    return jnp.concatenate([block[:, h * HD : (h + 1) * HD] for h in range(HEADS)], axis=0)


def to_columns(rows):
    return jnp.concatenate([rows[h * CL : (h + 1) * CL] for h in range(HEADS)], axis=1)


def norm(raw, gain):
    raw = raw.astype(F32)
    reciprocal = lax.rsqrt(jnp.mean(raw * raw, axis=-1, keepdims=True) + EPS)
    unit = raw * reciprocal
    return unit, reciprocal, unit * gain


def norm_back(upstream, unit, reciprocal, gain):
    scaled = upstream * gain
    return reciprocal * (scaled - unit * jnp.mean(unit * scaled, axis=-1, keepdims=True))


def attention_kernel(
    live,
    prompts,
    q_ref,
    k_ref,
    v_ref,
    out_grad_ref,
    a_ref,
    b_ref,
    query_gain_ref,
    key_gain_ref,
    attended_ref,
    dq_ref,
    dk_ref,
    dv_ref,
    grad_a_ref,
    grad_b_ref,
    gain_ref,
    pool_keys,
    pool_values,
    pool_units,
    key_sum,
    value_sum,
):
    head, slot = pl.program_id(0), pl.program_id(1)
    query_gain, key_gain = query_gain_ref[...], key_gain_ref[...]

    @pl.when((slot == 0) & (head == 0))
    def _():
        gain_ref[...] = jnp.zeros_like(gain_ref)

    @pl.when(slot == 0)
    def _():
        a = a_ref[...].astype(F32).reshape(16, BLOCK, HD)
        b = b_ref[...].astype(F32)
        for p in range(2):
            rows = slice(24 * p, 24 * p + 24)
            unit, _, normed = norm(a[:, rows].reshape(PL, HD), key_gain)
            pool_units[p] = unit
            pool_keys[p] = normed.astype(BF16)
            pool_values[p] = jnp.concatenate(
                [b[xx, yy, rows] for yy in range(4) for xx in range(4)], axis=0
            ).astype(BF16)
        key_sum[...] = jnp.zeros_like(key_sum)
        value_sum[...] = jnp.zeros_like(value_sum)

    alive = slot < live[0]
    prompt = prompts[slot]

    @pl.when(jnp.logical_not(alive))
    def _():
        attended_ref[...] = jnp.zeros_like(attended_ref)
        dq_ref[...] = jnp.zeros_like(dq_ref)
        dk_ref[...] = jnp.zeros_like(dk_ref)
        dv_ref[...] = jnp.zeros_like(dv_ref)

    @pl.when(alive)
    def _():
        unit_q, recip_q, normed_q = norm(to_rows(q_ref[...]), query_gain)
        queries = normed_q.astype(BF16)
        unit_k, recip_k, normed_k = norm(k_ref[...], key_gain)
        keys = jnp.concatenate([pool_keys[prompt], normed_k.astype(BF16)], axis=0)
        values = jnp.concatenate([pool_values[prompt], v_ref[...]], axis=0)
        grads = to_rows(out_grad_ref[...])
        scores = dot(queries, keys, 1, 1)
        token = lax.broadcasted_iota(jnp.int32, scores.shape, 0) % CL
        column = lax.broadcasted_iota(jnp.int32, scores.shape, 1) - PL
        scores = jnp.where(column <= token, scores, -jnp.inf)
        high = jnp.max(scores, axis=-1, keepdims=True)
        weights = jnp.exp2((scores - high) * EXPONENT)
        p = weights * (1.0 / jnp.sum(weights, axis=-1, keepdims=True))
        p_half = p.astype(BF16)
        p_rest = (p - p_half.astype(F32)).astype(BF16)
        attended = (dot(p_half, values, 1, 0) + dot(p_rest, values, 1, 0)).astype(BF16)
        attended_ref[...] = to_columns(attended)
        delta = jnp.sum(grads.astype(F32) * attended.astype(F32), axis=-1, keepdims=True)
        ds = (p * (dot(grads, values, 1, 1) - delta)).astype(BF16)
        dqn = dot(ds, keys, 1, 0) * SCALE
        dvn = dot(p_half, grads, 0, 0)
        dkn = dot(ds, queries, 0, 0) * SCALE
        gain_ref[0:1] += jnp.sum(dqn * unit_q, axis=0, keepdims=True)
        dq_ref[...] = to_columns(norm_back(dqn, unit_q, recip_q, query_gain).astype(BF16))
        key_sum[prompt] += dkn[:PL]
        value_sum[prompt] += dvn[:PL]
        own = dkn[PL:]
        gain_ref[1:2] += jnp.sum(own * unit_k, axis=0, keepdims=True)
        dk_ref[...] = norm_back(own, unit_k, recip_k, key_gain).astype(BF16)
        dv_ref[...] = dvn[PL:].astype(BF16)

    @pl.when(slot == pl.num_programs(1) - 1)
    def _():
        sums = key_sum[...]
        terms = (sums * pool_units[...]).reshape(2 * PL, HD)
        gain_ref[1:2] += jnp.sum(terms, axis=0, keepdims=True)
        sums = sums.reshape(2, 4, 4, 24, HD)
        grad_a_ref[...] = jnp.concatenate([sums[0], sums[1]], axis=2).astype(BF16)
        sums = value_sum[...].reshape(2, 4, 4, 24, HD)
        for xx in range(4):
            for yy in range(4):
                grad_b_ref[xx, yy] = jnp.concatenate(
                    [sums[0, yy, xx], sums[1, yy, xx]], axis=0
                ).astype(BF16)


def attention(live, prompts, q, k, v, out_grad, a, b, query_gain, key_gain):
    wide = pl.BlockSpec((CL, HEADS * HD), lambda head, slot, *_: (slot, head))
    narrow = pl.BlockSpec((CL, HD), lambda head, slot, *_: (slot, head))
    pool = pl.BlockSpec((4, 4, BLOCK, HD), lambda head, slot, *_: (0, 0, 0, head))
    row = pl.BlockSpec((1, HD), lambda head, slot, *_: (0, 0))
    shape = jax.ShapeDtypeStruct
    heads, slots = k.shape[1] // HD, k.shape[0] // CL
    return pl.pallas_call(
        attention_kernel,
        grid_spec=pltpu.PrefetchScalarGridSpec(
            num_scalar_prefetch=2,
            grid=(heads, slots),
            in_specs=[wide, narrow, narrow, wide, pool, pool, row, row],
            out_specs=[
                wide,
                wide,
                narrow,
                narrow,
                pool,
                pool,
                pl.BlockSpec((8, HD), lambda head, slot, *_: (0, 0)),
            ],
            scratch_shapes=[
                pltpu.VMEM((2, PL, HD), BF16),
                pltpu.VMEM((2, PL, HD), BF16),
                pltpu.VMEM((2, PL, HD), F32),
                pltpu.VMEM((2, PL, HD), F32),
                pltpu.VMEM((2, PL, HD), F32),
            ],
        ),
        out_shape=[
            shape(q.shape, BF16),
            shape(q.shape, BF16),
            shape(k.shape, BF16),
            shape(k.shape, BF16),
            shape(a.shape, BF16),
            shape(a.shape, BF16),
            shape((8, HD), F32),
        ],
        compiler_params=pltpu.CompilerParams(vmem_limit_bytes=48 << 20),
    )(live, prompts, q, k, v, out_grad, a, b, query_gain, key_gain)


def reduce_kernel(
    a_ref,
    b_ref,
    gain_ref,
    keys_ref,
    key_gain_ref,
    dk_ref,
    dv_ref,
    total_ref,
    first_in,
    second_out,
    second_in,
    last_out,
    last_in,
    y_gains,
    x_gains,
    z_gains,
    first_send,
    first_recv,
    second_send,
    second_recv,
    last_send,
    last_recv,
    y_send,
    y_recv,
    x_send,
    x_recv,
    z_send,
    z_recv,
):
    z, y, x, tp = place()
    here = (z * 4 + tp) % 16

    def at(zz, yy, xx):
        return (zz * 16 + yy * 4 + xx, tp)

    z_peers = [at((z + d) % 4, y, x) for d in (1, 2, 3)]
    y_peers = [at(z, (y + d) % 4, x) for d in (1, 2, 3)]
    x_peers = [at(z, y, (x + d) % 4) for d in (1, 2, 3)]
    around = [(here + d) % 16 for d in range(1, 16)]
    all_peers = [(other // 4 * 16 + y * 4 + x, other % 4) for other in around]
    greet(y_peers + x_peers + all_peers)
    y_gains[y] = gain_ref[...]
    gain_copies = [
        send(y_gains.at[y], y_gains.at[y], y_send.at[d], y_recv.at[d], y_peers[d]) for d in range(3)
    ]
    halves = ((a_ref, y, x, y_peers, x_peers), (b_ref, x, y, x_peers, y_peers))
    firsts = [[], []]
    for step in range(4):
        for half, (ref, slow, fast, far, near) in enumerate(halves):
            chunk = (fast + 1 + step) % 4
            firsts[half].append(
                [
                    send(
                        ref.at[(slow + 1 + d) % 4, chunk],
                        first_in.at[half, d, step],
                        first_send.at[half, d, step],
                        first_recv.at[half, d, step],
                        far[d],
                    )
                    for d in range(3)
                ]
            )
    seconds = [[], []]
    own = [None, None]
    for step in range(4):
        for half, (ref, slow, fast, far, near) in enumerate(halves):
            for copy in firsts[half][step]:
                copy.wait_recv()
            part = ref[slow, (fast + 1 + step) % 4].astype(F32)
            for d in range(3):
                part += first_in[half, d, step].astype(F32)
            if step < 3:
                second_out[half, step] = part.astype(BF16)
                seconds[half].append(
                    send(
                        second_out.at[half, step],
                        second_in.at[half, step],
                        second_send.at[half, step],
                        second_recv.at[half, step],
                        near[step],
                    )
                )
            else:
                own[half] = part
    for copy in gain_copies:
        copy.wait_recv()
    x_gains[x] = (y_gains[0] + y_gains[1]) + (y_gains[2] + y_gains[3])
    more = [
        send(x_gains.at[x], x_gains.at[x], x_send.at[d], x_recv.at[d], x_peers[d]) for d in range(3)
    ]
    for copy in more:
        copy.wait_recv()
    gain_copies += more
    z_gains[here] = (x_gains[0] + x_gains[1]) + (x_gains[2] + x_gains[3])
    more = [
        send(z_gains.at[here], z_gains.at[here], z_send.at[d], z_recv.at[d], all_peers[d])
        for d in range(15)
    ]
    for half in range(2):
        for step in range(3):
            seconds[half][step].wait_recv()
            own[half] += second_in[half, step].astype(F32)
    for zz in range(4):
        for half in range(2):
            last_out[zz, :OWN, half * 2 * HD : (half + 1) * 2 * HD] = own[half][
                zz * OWN : (zz + 1) * OWN
            ]
        last_out[zz, OWN:] = jnp.zeros((PAD - OWN, 4 * HD), F32)
    lasts = [
        send(last_out.at[(z + 1 + d) % 4], last_in.at[d], last_send.at[d], last_recv.at[d], z_peers[d])
        for d in range(3)
    ]
    for copy in more:
        copy.wait_recv()
    gain_copies += more
    total = z_gains[0]
    for other in range(1, 16):
        total += z_gains[other]
    total_ref[...] = total
    for copy in lasts:
        copy.wait_recv()
    mine = last_out[z]
    for d in range(3):
        mine += last_in[d]
    mine = mine[:OWN]
    dv_ref[...] = mine[:, 2 * HD :]
    key_gain = key_gain_ref[...]
    for head in range(2):
        columns = slice(head * HD, (head + 1) * HD)
        unit, reciprocal, _ = norm(keys_ref[:, columns], key_gain)
        dk_ref[:, columns] = norm_back(mine[:, columns], unit, reciprocal, key_gain)
    for copy in gain_copies + lasts + seconds[0] + seconds[1]:
        copy.wait_send()
    for half in range(2):
        for step in range(4):
            for copy in firsts[half][step]:
                copy.wait_send()


def reduce(a, b, gains, keys, key_gain):
    vmem = pl.BlockSpec(memory_space=pltpu.VMEM)
    dma = pltpu.SemaphoreType.DMA
    shape = jax.ShapeDtypeStruct(keys.shape, F32)
    return pl.pallas_call(
        reduce_kernel,
        out_shape=[shape, shape, jax.ShapeDtypeStruct((8, HD), F32)],
        in_specs=[vmem] * 5,
        out_specs=[vmem] * 3,
        scratch_shapes=[
            pltpu.VMEM((2, 3, 4, BLOCK, 2 * HD), BF16),
            pltpu.VMEM((2, 3, BLOCK, 2 * HD), BF16),
            pltpu.VMEM((2, 3, BLOCK, 2 * HD), BF16),
            pltpu.VMEM((4, PAD, 4 * HD), F32),
            pltpu.VMEM((3, PAD, 4 * HD), F32),
            pltpu.VMEM((4, 8, HD), F32),
            pltpu.VMEM((4, 8, HD), F32),
            pltpu.VMEM((16, 8, HD), F32),
            dma((2, 3, 4)),
            dma((2, 3, 4)),
            dma((2, 3)),
            dma((2, 3)),
            dma((3,)),
            dma((3,)),
            dma((3,)),
            dma((3,)),
            dma((3,)),
            dma((3,)),
            dma((15,)),
            dma((15,)),
        ],
        compiler_params=pltpu.CompilerParams(collective_id=1, has_side_effects=True),
    )(a, b, gains, keys, key_gain)


def local(
    comp_queries,
    comp_keys,
    comp_values,
    prompt_keys,
    prompt_values,
    query_gain,
    key_gain,
    out_grad,
    live_counts,
    slot_prompts,
):
    query_gain, key_gain = query_gain.reshape(1, HD), key_gain.reshape(1, HD)
    pool_a, pool_b = gather(prompt_keys, prompt_values)
    attended, dq, dk, dv, grad_a, grad_b, gains = attention(
        live_counts,
        slot_prompts,
        comp_queries,
        comp_keys,
        comp_values,
        out_grad,
        pool_a,
        pool_b,
        query_gain,
        key_gain,
    )
    prompt_dk, prompt_dv, gains = reduce(grad_a, grad_b, gains, prompt_keys, key_gain)
    return (attended, dq, dk, dv, prompt_dk, prompt_dv, gains[0], gains[1])


def solution(mesh):
    both, grp = P("grp", "tp"), P("grp")
    return jax.shard_map(
        local,
        mesh=mesh,
        in_specs=(both, both, both, both, both, P(), P(), both, grp, grp),
        out_specs=(both, both, both, both, both, both, P(), P()),
        check_vma=False,
    )
```

```python
import functools
import math
import types

import jax
import jax.numpy as jnp
from jax import lax
from jax.experimental import pallas as pl
from jax.experimental.pallas import tpu as pltpu
from jax.sharding import PartitionSpec as P

HD = 128
CL = 64
PL = 384
HEADS = 8
OWN = 12
PAD = 16
BLOCK = 48
EPS = 1e-6
SCALE = 1.0 / math.sqrt(HD)
EXPONENT = SCALE * math.log2(math.e)
F32 = jnp.float32
BF16 = jnp.bfloat16
MESH = pl.DeviceIdType.MESH


def place():
    grp = lax.axis_index("grp")
    return grp // 16, (grp // 4) % 4, grp % 4, lax.axis_index("tp")


def greet(targets):
    barrier = pltpu.get_barrier_semaphore()
    for target in targets:
        pl.semaphore_signal(barrier, inc=1, device_id=target, device_id_type=MESH)
    pl.semaphore_wait(barrier, len(targets))


def send(source, target_ref, send_sem, recv_sem, target):
    copy = pltpu.make_async_remote_copy(
        src_ref=source,
        dst_ref=target_ref,
        send_sem=send_sem,
        recv_sem=recv_sem,
        device_id=target,
        device_id_type=MESH,
    )
    copy.start()
    return copy


def dot(left, right, over_left, over_right):
    return lax.dot_general(
        left, right, (((over_left,), (over_right,)), ((), ())), preferred_element_type=F32
    )


def to_rows(block):
    return jnp.concatenate([block[:, h * HD : (h + 1) * HD] for h in range(HEADS)], axis=0)


def to_columns(rows):
    return jnp.concatenate([rows[h * CL : (h + 1) * CL] for h in range(HEADS)], axis=1)


def norm(raw, gain):
    raw = raw.astype(F32)
    reciprocal = lax.rsqrt(jnp.mean(raw * raw, axis=-1, keepdims=True) + EPS)
    unit = raw * reciprocal
    return unit, reciprocal, unit * gain


def norm_back(upstream, unit, reciprocal, gain):
    scaled = upstream * gain
    return reciprocal * (scaled - unit * jnp.mean(unit * scaled, axis=-1, keepdims=True))


class Unit:
    def __init__(self, refs, head, slot):
        self.refs, self.head, self.slot = refs, head, slot
        self.index = head * 4 + slot
        self.rows = slice(slot * CL, (slot + 1) * CL)
        self.wide = slice(head * HEADS * HD, (head + 1) * HEADS * HD)
        self.narrow = slice(head * HD, (head + 1) * HD)

    def scalars(self):
        refs = self.refs
        self.alive = (self.slot < refs.live[0]).astype(F32)
        prompt = refs.prompts[self.slot]
        self.prompt = prompt
        self.shares = [self.alive * (prompt == p).astype(F32) for p in range(2)]

    def normalize(self):
        refs = self.refs
        unit, reciprocal, normed = norm(
            to_rows(refs.q[self.rows, self.wide]), refs.query_gain
        )
        refs.units_q[self.index] = unit
        refs.recips_q[self.index] = jnp.broadcast_to(reciprocal, unit.shape)
        refs.queries[self.index] = normed.astype(BF16)

    def load(self):
        refs = self.refs
        self.queries = refs.queries[self.index]
        self.unit_k, self.recip_k, normed = norm(
            refs.k[self.rows, self.narrow], refs.key_gain
        )
        self.keys = jnp.concatenate(
            [refs.pool_keys[self.head, self.prompt], normed.astype(BF16)], axis=0
        )
        self.values = jnp.concatenate(
            [refs.pool_values[self.head, self.prompt], refs.v[self.rows, self.narrow]], axis=0
        )
        self.grads = to_rows(refs.out_grad[self.rows, self.wide])

    def scores(self):
        self.s = dot(self.queries, self.keys, 1, 1)

    def softmax(self):
        s = self.s
        own_shape = (s.shape[0], CL)
        token = lax.broadcasted_iota(jnp.int32, own_shape, 0) % CL
        column = lax.broadcasted_iota(jnp.int32, own_shape, 1)
        own = jnp.where(column <= token, s[:, PL:], -jnp.inf)
        s = jnp.concatenate([s[:, :PL], own], axis=1)
        weights = jnp.exp2((s - jnp.max(s, axis=-1, keepdims=True)) * EXPONENT)
        self.p = weights * (1.0 / jnp.sum(weights, axis=-1, keepdims=True))
        self.p_half = self.p.astype(BF16)
        self.p_rest = (self.p - self.p_half.astype(F32)).astype(BF16)

    def dp(self):
        self.dp_ = dot(self.grads, self.values, 1, 1)

    def out(self):
        refs = self.refs
        total = dot(self.p_half, self.values, 1, 0) + dot(self.p_rest, self.values, 1, 0)
        self.attended = (total * self.alive).astype(BF16)
        self.emit(refs.held_attended, refs.out_attended, 0, self.wide, to_columns(self.attended))

    def ds(self):
        delta = jnp.sum(
            self.grads.astype(F32) * self.attended.astype(F32), axis=-1, keepdims=True
        )
        self.ds_ = (self.p * (self.dp_ - delta)).astype(BF16)

    def dv(self):
        self.dv_ = dot(self.grads.T, self.p_half, 1, 0)

    def dk(self):
        self.dk_ = dot(self.queries.T, self.ds_, 1, 0)

    def add(self, sums, grad, scale):
        for p in range(2):
            term = grad[:, :PL] * (self.shares[p] * scale)
            if self.slot > 0:
                term += sums[self.head, p]
            sums[self.head, p] = term

    def dq(self):
        self.dq_ = dot(self.ds_, self.keys, 1, 0) * (SCALE * self.alive)

    def finish(self):
        refs = self.refs
        unit, reciprocal = refs.units_q[self.index], refs.recips_q[self.index]
        back = norm_back(self.dq_, unit, reciprocal, refs.query_gain)
        self.emit(refs.held_dq, refs.out_dq, 1, self.wide, to_columns(back.astype(BF16)))

    def own(self):
        refs = self.refs
        own = self.dk_[:, PL:].T * (SCALE * self.alive)
        add_gains(refs, own, self.keys[PL:], self.unit_k)
        back = norm_back(own, self.unit_k, self.recip_k, refs.key_gain)
        self.emit(refs.held_dk, refs.out_dk, 2, self.narrow, back.astype(BF16))
        self.emit(refs.held_dv, refs.out_dv, 3, self.narrow, (self.dv_[:, PL:].T * self.alive).astype(BF16))

    def emit(self, held, target, which, columns, block):
        held[self.rows, columns] = block
        copy = pltpu.make_async_copy(
            held.at[self.rows, columns],
            target.at[self.rows, columns],
            self.refs.out_sem.at[which, self.index],
        )
        copy.start()
        self.refs.copies.append(copy)


def add_gains(refs, grads, keys, units):
    refs.gain[0:1] += jnp.sum(grads * keys.astype(F32), axis=0, keepdims=True) / refs.query_gain
    refs.gain[1:2] += jnp.sum(grads * units, axis=0, keepdims=True)


def unpack_pool(refs, head):
    a = refs.pool_a[head].astype(F32).reshape(16, BLOCK, HD)
    b = refs.pool_b[head].astype(F32)
    for p in range(2):
        rows = slice(24 * p, 24 * p + 24)
        unit, _, normed = norm(a[:, rows].reshape(PL, HD), refs.key_gain)
        refs.pool_units[head, p] = unit
        refs.pool_keys[head, p] = normed.astype(BF16)
        refs.pool_values[head, p] = jnp.concatenate(
            [b[xx, yy, rows] for yy in range(4) for xx in range(4)], axis=0
        ).astype(BF16)


def pack_keys(refs, head):
    sums = [refs.key_sum[head, p].T for p in range(2)]
    for p in range(2):
        add_gains(refs, sums[p], refs.pool_keys[head, p], refs.pool_units[head, p])
    sums = [total.reshape(4, 4, 24, HD) for total in sums]
    refs.grad_a[head] = jnp.concatenate(sums, axis=2).astype(BF16)


def pack_values(refs, head):
    sums = [refs.value_sum[head, p].T.reshape(4, 4, 24, HD) for p in range(2)]
    for xx in range(4):
        for yy in range(4):
            refs.grad_b[head, xx, yy] = jnp.concatenate(
                [total[yy, xx] for total in sums], axis=0
            ).astype(BF16)


class Links:
    def __init__(self, refs):
        self.refs = refs
        z, y, x, tp = place()
        self.z, self.y, self.x, self.tp = z, y, x, tp
        self.here = z * 4 + tp

        def at(zz, yy, xx):
            return (zz * 16 + yy * 4 + xx, tp)

        turns = (1, 2, 3)
        self.z_peers = [at((z + d) % 4, y, x) for d in turns]
        self.y_peers = [at(z, (y + d) % 4, x) for d in turns]
        self.x_peers = [at(z, y, (x + d) % 4) for d in turns]
        self.spot = y * 4 + x
        plane = [(self.spot + d) % 16 for d in range(1, 16)]
        self.plane = [(z * 16 + spot, tp) for spot in plane]
        around = [(self.here + d) % 16 for d in range(1, 16)]
        self.around = [(other // 4 * 16 + self.spot, other % 4) for other in around]
        places = [[(z * 4 + fast + d) % 16 for d in range(1, 16)] for fast in (x, y)]
        self.others = places
        self.near = (
            [at(other // 4, y, other % 4) for other in places[0]],
            [at(other // 4, other % 4, x) for other in places[1]],
        )
        self.sent = []
        self.halves = ((y, x, self.y_peers), (x, y, self.x_peers))
        self.beside = (self.x_peers, self.y_peers)
        self.nears, self.far, self.firsts, self.lasts = {}, {}, {}, {}

    def greeted(self):
        z, y, x, turns = self.z, self.y, self.x, (1, 2, 3)
        spots = [(y, (x + d) % 4) for d in turns] + [((y + d) % 4, x) for d in turns]
        apart = [
            ((z + d) % 4 * 16 + yy * 4 + xx, self.tp) for d in turns for yy, xx in spots
        ]
        return self.plane + self.around + apart

    def send(self, *args):
        copy = send(*args)
        self.sent.append(copy)
        return copy

    def pool(self, half):
        return self.refs.pool_b if half else self.refs.pool_a

    def columns(self):
        refs, z = self.refs, self.z
        mine = jnp.concatenate([refs.keys[...], refs.values[...]], axis=1).astype(F32)
        mine = jnp.concatenate([mine, jnp.zeros((PAD - OWN, 4 * HD), F32)], axis=0)
        refs.columns[z] = mine.astype(BF16)
        ref = refs.columns.at[z]
        self.z_copies = [
            self.send(ref, ref, refs.z_send.at[d], refs.z_recv.at[d], self.z_peers[d])
            for d in range(3)
        ]

    def block(self):
        refs = self.refs
        for copy in self.z_copies:
            copy.wait_recv()
        block = jnp.concatenate(
            [refs.columns[zz].astype(F32)[:OWN] for zz in range(4)], axis=0
        ).astype(BF16)
        for head in range(2):
            for half, (slow, fast, far) in enumerate(self.halves):
                column = (half * 2 + head) * HD
                self.pool(half)[head, slow, fast] = block[:, column : column + HD]
        for head in range(2):
            for half, (slow, fast, far) in enumerate(self.halves):
                ref = self.pool(half).at[head, slow, fast]
                sems = refs.near_send, refs.near_recv
                self.nears[head, half] = [
                    self.send(ref, ref, sems[0].at[head, half, d], sems[1].at[head, half, d], self.beside[half][d])
                    for d in range(3)
                ]

    def forward_all(self):
        for head in range(2):
            for half, (slow, fast, far) in enumerate(self.halves):
                for copy in self.nears[head, half]:
                    copy.wait_recv()
                ref = self.pool(half).at[head, slow]
                sems = self.refs.far_send, self.refs.far_recv
                self.far[head, half] = [
                    self.send(
                        ref, ref, sems[0].at[head, half, d], sems[1].at[head, half, d], far[d]
                    )
                    for d in range(3)
                ]

    def arrived(self, head):
        for half in range(2):
            for copy in self.far[head, half]:
                copy.wait_recv()

    def grad(self, half):
        return self.refs.grad_b if half else self.refs.grad_a

    def first(self, head, half):
        slow, fast, far = self.halves[half]
        sems = self.refs.first_send, self.refs.first_recv
        self.firsts[head, half] = [
            self.send(
                self.grad(half).at[head, (slow + 1 + d) % 4],
                self.refs.first_in.at[head, half, d],
                sems[0].at[head, half, d],
                sems[1].at[head, half, d],
                far[d],
            )
            for d in range(3)
        ]

    def second(self, head, half):
        refs = self.refs
        slow, fast, far = self.halves[half]
        for copy in self.firsts[head, half]:
            copy.wait_recv()
        pad = jnp.zeros((PAD - OWN, HD), F32)
        for place in range(4):
            part = self.grad(half)[head, slow, place].astype(F32)
            for d in range(3):
                part += refs.first_in[head, half, d, place].astype(F32)
            for zz in range(4):
                piece = jnp.concatenate([part[zz * OWN : (zz + 1) * OWN], pad], axis=0)
                refs.own_sum[head, half, zz * 4 + place] = piece
                refs.last_out[head, half, zz * 4 + place] = piece.astype(BF16)
        self.lasts[head, half] = [
            self.send(
                refs.last_out.at[head, half, other],
                refs.last_in.at[head, half, d],
                refs.last_send.at[head, half, d],
                refs.last_recv.at[head, half, d],
                peer,
            )
            for d, (other, peer) in enumerate(zip(self.others[half], self.near[half]))
        ]

    def total(self, head, half):
        refs = self.refs
        slow, fast, far = self.halves[half]
        for copy in self.lasts[head, half]:
            copy.wait_recv()
        total = refs.own_sum[head, half, self.z * 4 + fast]
        total += jnp.sum(refs.last_in[head, half].astype(F32), axis=0)
        return total[:OWN]

    def around_gains(self):
        refs = self.refs
        refs.around_gains[self.here] = refs.gain[...]
        ref = refs.around_gains.at[self.here]
        self.gains = [
            self.send(ref, ref, refs.around_send.at[d], refs.around_recv.at[d], self.around[d])
            for d in range(15)
        ]

    def plane_gains(self):
        refs = self.refs
        for copy in self.gains:
            copy.wait_recv()
        refs.plane_gains[self.spot] = jnp.sum(refs.around_gains[...], axis=0)
        ref = refs.plane_gains.at[self.spot]
        self.gains = [
            self.send(ref, ref, refs.plane_send.at[d], refs.plane_recv.at[d], self.plane[d])
            for d in range(15)
        ]

    def total_gains(self):
        for copy in self.gains:
            copy.wait_recv()
        return jnp.sum(self.refs.plane_gains[...], axis=0)


DEFERRED = 2


def scratch_of(shapes):
    vmem, dma = pltpu.VMEM, pltpu.SemaphoreType.DMA
    wide, narrow, prompt = shapes
    return dict(
        keys=vmem(prompt, BF16),
        values=vmem(prompt, BF16),
        query_gain=vmem((1, HD), F32),
        key_gain=vmem((1, HD), F32),
        q=vmem(wide, BF16),
        k=vmem(narrow, BF16),
        v=vmem(narrow, BF16),
        out_grad=vmem(wide, BF16),
        live=pltpu.SMEM((1,), jnp.int32),
        prompts=pltpu.SMEM((4,), jnp.int32),
        in_sem=dma((10,)),
        units_q=vmem((8, HEADS * CL, HD), F32),
        recips_q=vmem((8, HEADS * CL, HD), F32),
        queries=vmem((8, HEADS * CL, HD), BF16),
        pool_keys=vmem((2, 2, PL, HD), BF16),
        pool_values=vmem((2, 2, PL, HD), BF16),
        pool_units=vmem((2, 2, PL, HD), F32),
        key_sum=vmem((2, 2, HD, PL), F32),
        value_sum=vmem((2, 2, HD, PL), F32),
        held_attended=vmem(wide, BF16),
        held_dq=vmem(wide, BF16),
        held_dk=vmem(narrow, BF16),
        held_dv=vmem(narrow, BF16),
        held_prompt_dk=vmem(prompt, F32),
        held_prompt_dv=vmem(prompt, F32),
        out_sem=dma((4, 8)),
        late_sem=dma((4,)),
        gain=vmem((8, HD), F32),
        columns=vmem((4, PAD, 4 * HD), BF16),
        pool_a=vmem((2, 4, 4, BLOCK, HD), BF16),
        pool_b=vmem((2, 4, 4, BLOCK, HD), BF16),
        grad_a=vmem((2, 4, 4, BLOCK, HD), BF16),
        grad_b=vmem((2, 4, 4, BLOCK, HD), BF16),
        first_in=vmem((2, 2, 3, 4, BLOCK, HD), BF16),
        own_sum=vmem((2, 2, 16, PAD, HD), F32),
        last_out=vmem((2, 2, 16, PAD, HD), BF16),
        last_in=vmem((2, 2, 15, PAD, HD), BF16),
        plane_gains=vmem((16, 8, HD), F32),
        around_gains=vmem((16, 8, HD), F32),
        total_gains=vmem((8, HD), F32),
        z_send=dma((3,)),
        z_recv=dma((3,)),
        near_send=dma((2, 2, 3)),
        near_recv=dma((2, 2, 3)),
        far_send=dma((2, 2, 3)),
        far_recv=dma((2, 2, 3)),
        first_send=dma((2, 2, 3)),
        first_recv=dma((2, 2, 3)),
        last_send=dma((2, 2, 15)),
        last_recv=dma((2, 2, 15)),
        plane_send=dma((15,)),
        plane_recv=dma((15,)),
        around_send=dma((15,)),
        around_recv=dma((15,)),
    )


def main_kernel(names, *refs):
    refs = types.SimpleNamespace(**dict(zip(names, refs)))
    moves = (
        (refs.in_keys, refs.keys),
        (refs.in_values, refs.values),
        (refs.in_query_gain, refs.query_gain),
        (refs.in_key_gain, refs.key_gain),
        (refs.in_q, refs.q),
        (refs.in_k, refs.k),
        (refs.in_v, refs.v),
        (refs.in_out_grad, refs.out_grad),
        (refs.in_live, refs.live),
        (refs.in_prompts, refs.prompts),
    )
    entering = [
        pltpu.make_async_copy(source, target, refs.in_sem.at[i])
        for i, (source, target) in enumerate(moves)
    ]
    for copy in entering:
        copy.start()
    links = Links(refs)
    greet(links.greeted())
    entering[0].wait()
    entering[1].wait()
    links.columns()
    for copy in entering[2:]:
        copy.wait()
    refs.query_gain, refs.key_gain = refs.query_gain[...], refs.key_gain[...]
    refs.gain[...] = jnp.zeros_like(refs.gain)
    refs.copies = []
    units = [Unit(refs, head, slot) for head in range(2) for slot in range(4)]
    for unit in units:
        unit.scalars()
    for unit in units[:4]:
        unit.normalize()
    links.block()
    links.forward_all()
    for unit in units[4:]:
        unit.normalize()
    count = len(units)
    links.arrived(0)
    unpack_pool(refs, 0)
    units[0].load()
    units[0].scores()
    for now in range(count + 1):
        unit = units[now] if now < count else None
        before = units[now - 1] if now > 0 else None
        if now + 1 < count:
            if now == 2:
                links.arrived(1)
                unpack_pool(refs, 1)
            units[now + 1].load()
            units[now + 1].scores()
        if unit:
            unit.softmax()
            unit.dp()
        if before:
            before.add(refs.value_sum, before.dv_, 1.0)
            if now % 4 == 0:
                pack_values(refs, before.head)
                links.first(before.head, 1)
            before.dk()
            before.add(refs.key_sum, before.dk_, SCALE)
            before.own()
            if now % 4 == 0:
                pack_keys(refs, before.head)
                links.first(before.head, 0)
        if unit:
            unit.out()
        if before and now <= DEFERRED:
            before.dq()
        if unit:
            unit.ds()
            unit.dv()
        if before and now <= DEFERRED:
            before.finish()
    links.around_gains()
    for unit in units[DEFERRED:]:
        unit.dq()
        unit.finish()
    for head in range(2):
        for half in (1, 0):
            links.second(head, half)
    links.plane_gains()
    late = []

    def leave(source, target):
        copy = pltpu.make_async_copy(source, target, refs.late_sem.at[len(late)])
        copy.start()
        late.append(copy)

    for copy in links.sent:
        copy.wait_send()
    for copy in refs.copies:
        copy.wait()
    for head in range(2):
        columns = slice(head * HD, (head + 1) * HD)
        refs.held_prompt_dv[:, columns] = links.total(head, 1)
        unit, reciprocal, _ = norm(refs.keys[:, columns], refs.key_gain)
        refs.held_prompt_dk[:, columns] = norm_back(
            links.total(head, 0), unit, reciprocal, refs.key_gain
        )
    leave(refs.held_prompt_dv, refs.out_prompt_dv)
    leave(refs.held_prompt_dk, refs.out_prompt_dk)
    refs.total_gains[...] = links.total_gains()
    leave(refs.total_gains.at[0:1], refs.out_query_total)
    leave(refs.total_gains.at[1:2], refs.out_key_total)
    for copy in late:
        copy.wait()


def main(**arrays):
    wide, narrow, prompt = (arrays[name].shape for name in ("in_q", "in_k", "in_keys"))
    scratch = scratch_of((wide, narrow, prompt))
    hbm = pl.BlockSpec(memory_space=pltpu.HBM)
    shape = jax.ShapeDtypeStruct
    outs = dict(
        out_attended=shape(wide, BF16),
        out_dq=shape(wide, BF16),
        out_dk=shape(narrow, BF16),
        out_dv=shape(narrow, BF16),
        out_prompt_dk=shape(prompt, F32),
        out_prompt_dv=shape(prompt, F32),
        out_query_total=shape((1, HD), F32),
        out_key_total=shape((1, HD), F32),
    )
    return pl.pallas_call(
        functools.partial(main_kernel, [*arrays, *outs, *scratch]),
        out_shape=list(outs.values()),
        in_specs=[hbm] * len(arrays),
        out_specs=[hbm] * len(outs),
        scratch_shapes=list(scratch.values()),
        compiler_params=pltpu.CompilerParams(
            collective_id=0, has_side_effects=True, vmem_limit_bytes=60 << 20
        ),
    )(*arrays.values())


def copy_kernel(*refs):
    count = (len(refs) - 1) // 3
    sources, targets, held = refs[:count], refs[count : 2 * count], refs[2 * count : 3 * count]
    sem = refs[-1]
    pairs = []
    for source, target, between in zip(sources, targets, held):
        rows = source.shape[0]
        piece = rows if rows < CL else CL
        for start in range(0, rows, piece):
            at, now = pl.ds(start, piece), len(pairs)
            entering = pltpu.make_async_copy(source.at[at], between.at[at], sem.at[0, now])
            leaving = pltpu.make_async_copy(between.at[at], target.at[at], sem.at[1, now])
            entering.start()
            pairs.append((entering, leaving))
    for entering, leaving in pairs:
        entering.wait()
        leaving.start()
    for entering, leaving in pairs:
        leaving.wait()


def copy_out(arrays):
    hbm = pl.BlockSpec(memory_space=pltpu.HBM)
    return pl.pallas_call(
        copy_kernel,
        out_shape=[jax.ShapeDtypeStruct(array.shape, array.dtype) for array in arrays],
        in_specs=[hbm] * len(arrays),
        out_specs=[hbm] * len(arrays),
        scratch_shapes=[pltpu.VMEM(array.shape, array.dtype) for array in arrays]
        + [pltpu.SemaphoreType.DMA((2, 32))],
        compiler_params=pltpu.CompilerParams(vmem_limit_bytes=60 << 20),
    )(*arrays)


def local(
    comp_queries,
    comp_keys,
    comp_values,
    prompt_keys,
    prompt_values,
    query_gain,
    key_gain,
    out_grad,
    live_counts,
    slot_prompts,
):
    results = main(
        in_keys=prompt_keys,
        in_values=prompt_values,
        in_query_gain=query_gain.reshape(1, HD),
        in_key_gain=key_gain.reshape(1, HD),
        in_q=comp_queries,
        in_k=comp_keys,
        in_v=comp_values,
        in_out_grad=out_grad,
        in_live=live_counts,
        in_prompts=slot_prompts,
    )
    *arrays, query_total, key_total = copy_out(results)
    return (*arrays, query_total.reshape(HD), key_total.reshape(HD))


def solution(mesh):
    both, grp = P("grp", "tp"), P("grp")
    return jax.shard_map(
        local,
        mesh=mesh,
        in_specs=(both, both, both, both, both, P(), P(), both, grp, grp),
        out_specs=(both, both, both, both, both, both, P(), P()),
        check_vma=False,
    )
```

```python
import functools
import math
import types

import jax
import jax.numpy as jnp
from jax import lax
from jax.experimental import pallas as pl
from jax.experimental.pallas import tpu as pltpu
from jax.sharding import PartitionSpec as P

HD = 128
CL = 64
PL = 384
HEADS = 8
OWN = 12
PAD = 16
BLOCK = 48
EPS = 1e-6
SCALE = 1.0 / math.sqrt(HD)
EXPONENT = SCALE * math.log2(math.e)
F32 = jnp.float32
BF16 = jnp.bfloat16
MESH = pl.DeviceIdType.MESH


def place():
    grp = lax.axis_index("grp")
    return grp // 16, (grp // 4) % 4, grp % 4, lax.axis_index("tp")


def greet(targets):
    barrier = pltpu.get_barrier_semaphore()
    for target in targets:
        pl.semaphore_signal(barrier, inc=1, device_id=target, device_id_type=MESH)
    return functools.partial(pl.semaphore_wait, barrier, len(targets))


def send(source, target_ref, send_sem, recv_sem, target):
    copy = pltpu.make_async_remote_copy(
        src_ref=source,
        dst_ref=target_ref,
        send_sem=send_sem,
        recv_sem=recv_sem,
        device_id=target,
        device_id_type=MESH,
    )
    copy.start()
    return copy


def dot(left, right, over_left, over_right):
    return lax.dot_general(
        left, right, (((over_left,), (over_right,)), ((), ())), preferred_element_type=F32
    )


def to_rows(block):
    return jnp.concatenate([block[:, h * HD : (h + 1) * HD] for h in range(HEADS)], axis=0)


def to_columns(rows):
    return jnp.concatenate([rows[h * CL : (h + 1) * CL] for h in range(HEADS)], axis=1)


def norm(raw, gain):
    raw = raw.astype(F32)
    reciprocal = lax.rsqrt(jnp.mean(raw * raw, axis=-1, keepdims=True) + EPS)
    unit = raw * reciprocal
    return unit, reciprocal, unit * gain


def norm_back(upstream, unit, reciprocal, gain):
    scaled = upstream * gain
    return reciprocal * (scaled - unit * jnp.mean(unit * scaled, axis=-1, keepdims=True))


class Unit:
    def __init__(self, refs, head, slot):
        self.refs, self.head, self.slot = refs, head, slot
        self.index = head * 4 + slot
        self.rows = slice(slot * CL, (slot + 1) * CL)
        self.wide = slice(head * HEADS * HD, (head + 1) * HEADS * HD)
        self.narrow = slice(head * HD, (head + 1) * HD)

    def scalars(self):
        refs = self.refs
        self.alive = (self.slot < refs.live[0]).astype(F32)
        prompt = refs.prompts[self.slot]
        self.prompt = prompt
        self.shares = [self.alive * (prompt == p).astype(F32) for p in range(2)]

    def prepare(self):
        refs = self.refs
        unit, reciprocal, normed = norm(
            to_rows(refs.q[self.rows, self.wide]), refs.query_gain
        )
        refs.units_q[self.index] = unit
        refs.recips_q[self.index] = jnp.broadcast_to(reciprocal, unit.shape)
        queries = normed.astype(BF16)
        refs.queries[self.index] = queries
        refs.queries_t[self.index] = queries.T
        refs.grads_t[self.index] = to_rows(refs.out_grad[self.rows, self.wide]).T
        unit, reciprocal, normed = norm(refs.k[self.rows, self.narrow], refs.key_gain)
        refs.units_k[self.index] = unit
        refs.recips_k[self.index] = jnp.broadcast_to(reciprocal, unit.shape)
        refs.own_keys[self.index] = normed.astype(BF16)

    def load(self):
        refs = self.refs
        self.queries = refs.queries[self.index]
        self.keys = jnp.concatenate(
            [refs.pool_keys[self.head, self.prompt], refs.own_keys[self.index]], axis=0
        )
        self.values = jnp.concatenate(
            [refs.pool_values[self.head, self.prompt], refs.v[self.rows, self.narrow]], axis=0
        )
        self.grads = to_rows(refs.out_grad[self.rows, self.wide])

    def scores(self):
        self.s = dot(self.queries, self.keys, 1, 1)

    def softmax(self):
        s = self.s
        own_shape = (s.shape[0], CL)
        token = lax.broadcasted_iota(jnp.int32, own_shape, 0) % CL
        column = lax.broadcasted_iota(jnp.int32, own_shape, 1)
        own = jnp.where(column <= token, s[:, PL:], -jnp.inf)
        s = jnp.concatenate([s[:, :PL], own], axis=1)
        weights = jnp.exp2((s - jnp.max(s, axis=-1, keepdims=True)) * EXPONENT)
        self.p = weights * (1.0 / jnp.sum(weights, axis=-1, keepdims=True))
        self.p_half = self.p.astype(BF16)
        self.p_rest = (self.p - self.p_half.astype(F32)).astype(BF16)

    def dp(self):
        self.dp_ = dot(self.grads, self.values, 1, 1)

    def out(self):
        refs = self.refs
        total = dot(self.p_half, self.values, 1, 0) + dot(self.p_rest, self.values, 1, 0)
        self.attended = (total * self.alive).astype(BF16)
        self.emit(refs.held_attended, refs.out_attended, 0, self.wide, to_columns(self.attended))

    def ds(self):
        delta = jnp.sum(
            self.grads.astype(F32) * self.attended.astype(F32), axis=-1, keepdims=True
        )
        self.ds_ = (self.p * (self.dp_ - delta)).astype(BF16)

    def dv(self):
        self.dv_ = dot(self.refs.grads_t[self.index], self.p_half, 1, 0)

    def dk(self):
        self.dk_ = dot(self.refs.queries_t[self.index], self.ds_, 1, 0)

    def add(self, sums, grad, scale):
        for p in range(2):
            term = grad[:, :PL] * (self.shares[p] * scale)
            if self.slot > 0:
                term += sums[self.head, p]
            sums[self.head, p] = term

    def dq(self):
        self.dq_ = dot(self.ds_, self.keys, 1, 0) * (SCALE * self.alive)

    def finish(self):
        refs = self.refs
        unit, reciprocal = refs.units_q[self.index], refs.recips_q[self.index]
        back = norm_back(self.dq_, unit, reciprocal, refs.query_gain)
        self.emit(refs.held_dq, refs.out_dq, 1, self.wide, to_columns(back.astype(BF16)))

    def own(self):
        refs = self.refs
        own = self.dk_[:, PL:].T * (SCALE * self.alive)
        terms = jnp.sum(own * self.keys[PL:].astype(F32), axis=0, keepdims=True)
        refs.gain[0:1] += terms / refs.query_gain
        refs.gain[1:2] += jnp.sum(own * refs.units_k[self.index], axis=0, keepdims=True)
        back = norm_back(
            own, refs.units_k[self.index], refs.recips_k[self.index], refs.key_gain
        )
        self.emit(refs.held_dk, refs.out_dk, 2, self.narrow, back.astype(BF16))
        self.emit(refs.held_dv, refs.out_dv, 3, self.narrow, (self.dv_[:, PL:].T * self.alive).astype(BF16))

    def emit(self, held, target, which, columns, block):
        held[self.rows, columns] = block
        copy = pltpu.make_async_copy(
            held.at[self.rows, columns],
            target.at[self.rows, columns],
            self.refs.out_sem.at[which, self.index],
        )
        copy.start()
        self.refs.copies.append(copy)


def unpack_pool(refs, head):
    a = refs.pool_a[:, :, head].astype(F32).reshape(16, BLOCK, HD)
    b = refs.pool_b[:, :, head].astype(F32)
    for p in range(2):
        rows = slice(24 * p, 24 * p + 24)
        refs.pool_keys[head, p] = a[:, rows].reshape(PL, HD).astype(BF16)
        refs.pool_values[head, p] = jnp.concatenate(
            [b[xx, yy, rows] for yy in range(4) for xx in range(4)], axis=0
        ).astype(BF16)


def pack_keys(refs, head):
    sums = [refs.key_sum[head, p].T for p in range(2)]
    terms = sum(sums[p] * refs.pool_keys[head, p].astype(F32) for p in range(2))
    terms = jnp.sum(terms, axis=0, keepdims=True)
    refs.gain[0:1] += terms / refs.query_gain
    refs.gain[1:2] += terms / refs.key_gain
    sums = [total.reshape(4, 4, 24, HD) for total in sums]
    refs.grad_a[head] = jnp.concatenate(sums, axis=2).astype(BF16)


def pack_values(refs, head):
    sums = [refs.value_sum[head, p].T.reshape(4, 4, 24, HD) for p in range(2)]
    for xx in range(4):
        for yy in range(4):
            refs.grad_b[head, xx, yy] = jnp.concatenate(
                [total[yy, xx] for total in sums], axis=0
            ).astype(BF16)


class Links:
    def __init__(self, refs):
        self.refs = refs
        z, y, x, tp = place()
        self.z, self.y, self.x, self.tp = z, y, x, tp
        self.here = z * 4 + tp

        def at(zz, yy, xx):
            return (zz * 16 + yy * 4 + xx, tp)

        turns = (1, 2, 3)
        self.z_peers = [at((z + d) % 4, y, x) for d in turns]
        self.y_peers = [at(z, (y + d) % 4, x) for d in turns]
        self.x_peers = [at(z, y, (x + d) % 4) for d in turns]
        self.spot = y * 4 + x
        plane = [(self.spot + d) % 16 for d in range(1, 16)]
        self.plane = [(z * 16 + spot, tp) for spot in plane]
        around = [(self.here + d) % 16 for d in range(1, 16)]
        self.around = [(other // 4 * 16 + self.spot, other % 4) for other in around]
        places = [[(z * 4 + fast + d) % 16 for d in range(1, 16)] for fast in (x, y)]
        self.others = places
        self.near = (
            [at(other // 4, y, other % 4) for other in places[0]],
            [at(other // 4, other % 4, x) for other in places[1]],
        )
        self.sent = []
        self.halves = ((y, x, self.y_peers), (x, y, self.x_peers))
        self.beside = (self.x_peers, self.y_peers)
        self.nears, self.far, self.firsts, self.lasts = {}, {}, {}, {}

    def greeted(self):
        grp = self.z * 16 + self.spot
        rest = [(grp, (self.tp + d) % 4) for d in (1, 2, 3)]
        return self.z_peers + self.y_peers + self.x_peers + rest

    def send(self, *args):
        copy = send(*args)
        self.sent.append(copy)
        return copy

    def pool(self, half):
        return self.refs.pool_b if half else self.refs.pool_a

    def prepare(self):
        refs = self.refs
        parts = [
            norm(refs.keys[:, head * HD : (head + 1) * HD], refs.key_gain)[2] for head in range(2)
        ]
        mine = jnp.concatenate(parts + [refs.values[...].astype(F32)], axis=1)
        mine = jnp.concatenate([mine, jnp.zeros((PAD - OWN, 4 * HD), F32)], axis=0)
        refs.columns[self.z] = mine.astype(BF16)

    def columns(self):
        refs = self.refs
        ref = refs.columns.at[self.z]
        self.z_copies = [
            self.send(ref, ref, refs.z_send.at[d], refs.z_recv.at[d], self.z_peers[d])
            for d in range(3)
        ]

    def block(self):
        refs = self.refs
        for copy in self.z_copies:
            copy.wait_recv()
        block = jnp.concatenate(
            [refs.columns[zz].astype(F32)[:OWN] for zz in range(4)], axis=0
        ).astype(BF16)
        for head in range(2):
            for half, (slow, fast, far) in enumerate(self.halves):
                column = (half * 2 + head) * HD
                self.pool(half)[slow, fast, head] = block[:, column : column + HD]
        for half, (slow, fast, far) in enumerate(self.halves):
            ref = self.pool(half).at[slow, fast]
            sems = refs.near_send, refs.near_recv
            self.nears[half] = [
                self.send(ref, ref, sems[0].at[half, d], sems[1].at[half, d], self.beside[half][d])
                for d in range(3)
            ]

    def forward(self, head):
        for half, (slow, fast, far) in enumerate(self.halves):
            if head == 0:
                for copy in self.nears[half]:
                    copy.wait_recv()
            ref = self.pool(half).at[slow, :, head]
            sems = self.refs.far_send, self.refs.far_recv
            self.far[head, half] = [
                self.send(ref, ref, sems[0].at[head, half, d], sems[1].at[head, half, d], far[d])
                for d in range(3)
            ]

    def arrived(self, head):
        for half in range(2):
            for copy in self.far[head, half]:
                copy.wait_recv()

    def grad(self, half):
        return self.refs.grad_b if half else self.refs.grad_a

    def first(self, head, half):
        slow, fast, far = self.halves[half]
        sems = self.refs.first_send, self.refs.first_recv
        self.firsts[head, half] = [
            self.send(
                self.grad(half).at[head, (slow + 1 + d) % 4],
                self.refs.first_in.at[head, half, d],
                sems[0].at[head, half, d],
                sems[1].at[head, half, d],
                far[d],
            )
            for d in range(3)
        ]

    def second(self, head, half):
        refs = self.refs
        slow, fast, far = self.halves[half]
        for copy in self.firsts[head, half]:
            copy.wait_recv()
        pad = jnp.zeros((PAD - OWN, HD), F32)
        for place in range(4):
            part = self.grad(half)[head, slow, place].astype(F32)
            for d in range(3):
                part += refs.first_in[head, half, d, place].astype(F32)
            for zz in range(4):
                piece = jnp.concatenate([part[zz * OWN : (zz + 1) * OWN], pad], axis=0)
                refs.own_sum[head, half, zz * 4 + place] = piece
                refs.last_out[head, half, zz * 4 + place] = piece.astype(BF16)
        self.lasts[head, half] = [
            self.send(
                refs.last_out.at[head, half, other],
                refs.last_in.at[head, half, d],
                refs.last_send.at[head, half, d],
                refs.last_recv.at[head, half, d],
                peer,
            )
            for d, (other, peer) in enumerate(zip(self.others[half], self.near[half]))
        ]

    def total(self, head, half):
        refs = self.refs
        slow, fast, far = self.halves[half]
        for copy in self.lasts[head, half]:
            copy.wait_recv()
        total = refs.own_sum[head, half, self.z * 4 + fast]
        total += jnp.sum(refs.last_in[head, half].astype(F32), axis=0)
        return total[:OWN]

    def around_gains(self):
        refs = self.refs
        refs.around_gains[self.here] = refs.gain[...]
        ref = refs.around_gains.at[self.here]
        self.gains = [
            self.send(ref, ref, refs.around_send.at[d], refs.around_recv.at[d], self.around[d])
            for d in range(15)
        ]

    def plane_gains(self):
        refs = self.refs
        for copy in self.gains:
            copy.wait_recv()
        refs.plane_gains[self.spot] = jnp.sum(refs.around_gains[...], axis=0)
        ref = refs.plane_gains.at[self.spot]
        self.gains = [
            self.send(ref, ref, refs.plane_send.at[d], refs.plane_recv.at[d], self.plane[d])
            for d in range(15)
        ]

    def total_gains(self):
        for copy in self.gains:
            copy.wait_recv()
        return jnp.sum(self.refs.plane_gains[...], axis=0)


DEFERRED = 0
PIECE = 64


def scratch_of(shapes):
    vmem, dma = pltpu.VMEM, pltpu.SemaphoreType.DMA
    wide, narrow, prompt = shapes
    return dict(
        keys=vmem(prompt, BF16),
        values=vmem(prompt, BF16),
        query_gain=vmem((1, HD), F32),
        key_gain=vmem((1, HD), F32),
        q=vmem(wide, BF16),
        k=vmem(narrow, BF16),
        v=vmem(narrow, BF16),
        out_grad=vmem(wide, BF16),
        live=pltpu.SMEM((1,), jnp.int32),
        prompts=pltpu.SMEM((4,), jnp.int32),
        in_sem=dma((10,)),
        units_q=vmem((8, HEADS * CL, HD), F32),
        recips_q=vmem((8, HEADS * CL, HD), F32),
        queries=vmem((8, HEADS * CL, HD), BF16),
        queries_t=vmem((8, HD, HEADS * CL), BF16),
        grads_t=vmem((8, HD, HEADS * CL), BF16),
        units_k=vmem((8, CL, HD), F32),
        recips_k=vmem((8, CL, HD), F32),
        own_keys=vmem((8, CL, HD), BF16),
        pool_keys=vmem((2, 2, PL, HD), BF16),
        pool_values=vmem((2, 2, PL, HD), BF16),
        key_sum=vmem((2, 2, HD, PL), F32),
        value_sum=vmem((2, 2, HD, PL), F32),
        held_attended=vmem(wide, BF16),
        held_dq=vmem(wide, BF16),
        held_dk=vmem(narrow, BF16),
        held_dv=vmem(narrow, BF16),
        held_prompt_dk=vmem(prompt, F32),
        held_prompt_dv=vmem(prompt, F32),
        out_sem=dma((4, 8)),
        late_sem=dma((4,)),
        gain=vmem((8, HD), F32),
        columns=vmem((4, PAD, 4 * HD), BF16),
        pool_a=vmem((4, 4, 2, BLOCK, HD), BF16),
        pool_b=vmem((4, 4, 2, BLOCK, HD), BF16),
        grad_a=vmem((2, 4, 4, BLOCK, HD), BF16),
        grad_b=vmem((2, 4, 4, BLOCK, HD), BF16),
        first_in=vmem((2, 2, 3, 4, BLOCK, HD), BF16),
        own_sum=vmem((2, 2, 16, PAD, HD), F32),
        last_out=vmem((2, 2, 16, PAD, HD), BF16),
        last_in=vmem((2, 2, 15, PAD, HD), BF16),
        plane_gains=vmem((16, 8, HD), F32),
        around_gains=vmem((16, 8, HD), F32),
        total_gains=vmem((8, HD), F32),
        z_send=dma((3,)),
        z_recv=dma((3,)),
        near_send=dma((2, 3)),
        near_recv=dma((2, 3)),
        far_send=dma((2, 2, 3)),
        far_recv=dma((2, 2, 3)),
        first_send=dma((2, 2, 3)),
        first_recv=dma((2, 2, 3)),
        last_send=dma((2, 2, 15)),
        last_recv=dma((2, 2, 15)),
        plane_send=dma((15,)),
        plane_recv=dma((15,)),
        around_send=dma((15,)),
        around_recv=dma((15,)),
    )


def main_kernel(names, *refs):
    refs = types.SimpleNamespace(**dict(zip(names, refs)))
    moves = (
        (refs.in_keys, refs.keys),
        (refs.in_values, refs.values),
        (refs.in_query_gain, refs.query_gain),
        (refs.in_key_gain, refs.key_gain),
        (refs.in_q, refs.q),
        (refs.in_k, refs.k),
        (refs.in_v, refs.v),
        (refs.in_out_grad, refs.out_grad),
        (refs.in_live, refs.live),
        (refs.in_prompts, refs.prompts),
    )
    entering = [
        pltpu.make_async_copy(source, target, refs.in_sem.at[i])
        for i, (source, target) in enumerate(moves)
    ]
    for copy in entering:
        copy.start()
    links = Links(refs)
    wait_for_greetings = greet(links.greeted())
    for copy in entering[:4]:
        copy.wait()
    refs.query_gain, refs.key_gain = refs.query_gain[...], refs.key_gain[...]
    links.prepare()
    wait_for_greetings()
    links.columns()
    for copy in entering[4:]:
        copy.wait()
    refs.gain[...] = jnp.zeros_like(refs.gain)
    refs.copies = []
    units = [Unit(refs, head, slot) for head in range(2) for slot in range(4)]
    for unit in units:
        unit.scalars()
    for unit in units[:4]:
        unit.prepare()
    links.block()
    links.forward(0)
    for unit in units[4:]:
        unit.prepare()
    links.forward(1)
    count = len(units)
    links.arrived(0)
    unpack_pool(refs, 0)
    units[0].load()
    units[0].scores()
    for now in range(count + 1):
        unit = units[now] if now < count else None
        before = units[now - 1] if now > 0 else None
        if now + 1 < count:
            if now == 2:
                links.arrived(1)
                unpack_pool(refs, 1)
            units[now + 1].load()
            units[now + 1].scores()
        if unit:
            unit.softmax()
            unit.dp()
        if unit:
            unit.out()
        if before:
            before.add(refs.value_sum, before.dv_, 1.0)
            if now % 4 == 0:
                pack_values(refs, before.head)
                links.first(before.head, 1)
            before.dk()
            before.add(refs.key_sum, before.dk_, SCALE)
            before.own()
            if now % 4 == 0:
                pack_keys(refs, before.head)
                links.first(before.head, 0)
        if before and now <= DEFERRED:
            before.dq()
        if unit:
            unit.ds()
            unit.dv()
        if before and now <= DEFERRED:
            before.finish()
    links.around_gains()
    for half in (1, 0):
        links.second(0, half)
    for unit in units[DEFERRED:]:
        unit.dq()
        unit.finish()
    for half in (1, 0):
        links.second(1, half)
    links.plane_gains()
    late = []

    def leave(source, target):
        copy = pltpu.make_async_copy(source, target, refs.late_sem.at[len(late)])
        copy.start()
        late.append(copy)

    for copy in links.sent:
        copy.wait_send()
    for copy in refs.copies:
        copy.wait()
    for head in range(2):
        columns = slice(head * HD, (head + 1) * HD)
        refs.held_prompt_dv[:, columns] = links.total(head, 1)
        unit, reciprocal, _ = norm(refs.keys[:, columns], refs.key_gain)
        refs.held_prompt_dk[:, columns] = norm_back(
            links.total(head, 0), unit, reciprocal, refs.key_gain
        )
    leave(refs.held_prompt_dv, refs.out_prompt_dv)
    leave(refs.held_prompt_dk, refs.out_prompt_dk)
    refs.total_gains[...] = links.total_gains()
    leave(refs.total_gains.at[0:1], refs.out_query_total)
    leave(refs.total_gains.at[1:2], refs.out_key_total)
    for copy in late:
        copy.wait()


def main(**arrays):
    wide, narrow, prompt = (arrays[name].shape for name in ("in_q", "in_k", "in_keys"))
    scratch = scratch_of((wide, narrow, prompt))
    hbm = pl.BlockSpec(memory_space=pltpu.HBM)
    shape = jax.ShapeDtypeStruct
    outs = dict(
        out_attended=shape(wide, BF16),
        out_dq=shape(wide, BF16),
        out_dk=shape(narrow, BF16),
        out_dv=shape(narrow, BF16),
        out_prompt_dk=shape(prompt, F32),
        out_prompt_dv=shape(prompt, F32),
        out_query_total=shape((1, HD), F32),
        out_key_total=shape((1, HD), F32),
    )
    return pl.pallas_call(
        functools.partial(main_kernel, [*arrays, *outs, *scratch]),
        out_shape=list(outs.values()),
        in_specs=[hbm] * len(arrays),
        out_specs=[hbm] * len(outs),
        scratch_shapes=list(scratch.values()),
        compiler_params=pltpu.CompilerParams(
            collective_id=0, has_side_effects=True, vmem_limit_bytes=60 << 20
        ),
    )(*arrays.values())


def copy_kernel(*refs):
    count = (len(refs) - 1) // 3
    sources, targets, held = refs[:count], refs[count : 2 * count], refs[2 * count : 3 * count]
    sem = refs[-1]
    pairs = []
    for source, target, between in zip(sources, targets, held):
        rows = source.shape[0]
        piece = min(rows, PIECE)
        for start in range(0, rows, piece):
            at, now = pl.ds(start, piece), len(pairs)
            entering = pltpu.make_async_copy(source.at[at], between.at[at], sem.at[0, now])
            leaving = pltpu.make_async_copy(between.at[at], target.at[at], sem.at[1, now])
            entering.start()
            pairs.append((entering, leaving))
    for entering, leaving in pairs:
        entering.wait()
        leaving.start()
    for entering, leaving in pairs:
        leaving.wait()


def copy_out(arrays):
    hbm = pl.BlockSpec(memory_space=pltpu.HBM)
    return pl.pallas_call(
        copy_kernel,
        out_shape=[jax.ShapeDtypeStruct(array.shape, array.dtype) for array in arrays],
        in_specs=[hbm] * len(arrays),
        out_specs=[hbm] * len(arrays),
        scratch_shapes=[pltpu.VMEM(array.shape, array.dtype) for array in arrays]
        + [pltpu.SemaphoreType.DMA((2, 32))],
        compiler_params=pltpu.CompilerParams(vmem_limit_bytes=60 << 20),
    )(*arrays)


def local(
    comp_queries,
    comp_keys,
    comp_values,
    prompt_keys,
    prompt_values,
    query_gain,
    key_gain,
    out_grad,
    live_counts,
    slot_prompts,
):
    results = main(
        in_keys=prompt_keys,
        in_values=prompt_values,
        in_query_gain=query_gain.reshape(1, HD),
        in_key_gain=key_gain.reshape(1, HD),
        in_q=comp_queries,
        in_k=comp_keys,
        in_v=comp_values,
        in_out_grad=out_grad,
        in_live=live_counts,
        in_prompts=slot_prompts,
    )
    *arrays, query_total, key_total = copy_out(results)
    return (*arrays, query_total.reshape(HD), key_total.reshape(HD))


def solution(mesh):
    both, grp = P("grp", "tp"), P("grp")
    return jax.shard_map(
        local,
        mesh=mesh,
        in_specs=(both, both, both, both, both, P(), P(), both, grp, grp),
        out_specs=(both, both, both, both, both, both, P(), P()),
        check_vma=False,
    )
```

```python
import functools
import math
import types

import jax
import jax.numpy as jnp
from jax import lax
from jax.experimental import pallas as pl
from jax.experimental.pallas import tpu as pltpu
from jax.sharding import PartitionSpec as P

HD = 128
CL = 64
PL = 384
HEADS = 8
OWN = 12
PAD = 16
BLOCK = 48
EPS = 1e-6
SCALE = 1.0 / math.sqrt(HD)
EXPONENT = SCALE * math.log2(math.e)
F32 = jnp.float32
BF16 = jnp.bfloat16
MESH = pl.DeviceIdType.MESH


def place():
    grp = lax.axis_index("grp")
    return grp // 16, (grp // 4) % 4, grp % 4, lax.axis_index("tp")


def greet(targets):
    barrier = pltpu.get_barrier_semaphore()
    for target in targets:
        pl.semaphore_signal(barrier, inc=1, device_id=target, device_id_type=MESH)
    return functools.partial(pl.semaphore_wait, barrier, len(targets))


def send(source, target_ref, send_sem, recv_sem, target):
    copy = pltpu.make_async_remote_copy(
        src_ref=source,
        dst_ref=target_ref,
        send_sem=send_sem,
        recv_sem=recv_sem,
        device_id=target,
        device_id_type=MESH,
    )
    copy.start()
    return copy


def dot(left, right, over_left, over_right):
    return lax.dot_general(
        left, right, (((over_left,), (over_right,)), ((), ())), preferred_element_type=F32
    )


def to_rows(block):
    return jnp.concatenate([block[:, h * HD : (h + 1) * HD] for h in range(HEADS)], axis=0)


def to_columns(rows):
    return jnp.concatenate([rows[h * CL : (h + 1) * CL] for h in range(HEADS)], axis=1)


def norm(raw, gain):
    raw = raw.astype(F32)
    reciprocal = lax.rsqrt(jnp.mean(raw * raw, axis=-1, keepdims=True) + EPS)
    unit = raw * reciprocal
    return unit, reciprocal, unit * gain


def norm_back(upstream, unit, reciprocal, gain):
    scaled = upstream * gain
    return reciprocal * (scaled - unit * jnp.mean(unit * scaled, axis=-1, keepdims=True))


class Unit:
    def __init__(self, refs, head, slot):
        self.refs, self.head, self.slot = refs, head, slot
        self.index = head * 4 + slot
        self.rows = slice(slot * CL, (slot + 1) * CL)
        self.wide = slice(head * HEADS * HD, (head + 1) * HEADS * HD)
        self.narrow = slice(head * HD, (head + 1) * HD)

    def scalars(self):
        refs = self.refs
        self.alive = (self.slot < refs.live[0]).astype(F32)
        prompt = refs.prompts[self.slot]
        self.prompt = prompt
        self.shares = [self.alive * (prompt == p).astype(F32) for p in range(2)]

    def prepare(self):
        refs = self.refs
        unit, reciprocal, normed = norm(
            to_rows(refs.q[self.rows, self.wide]), refs.query_gain
        )
        refs.units_q[self.index] = unit
        refs.recips_q[self.index] = jnp.broadcast_to(reciprocal, unit.shape)
        queries = normed.astype(BF16)
        refs.queries[self.index] = queries
        refs.queries_t[self.index] = queries.T
        refs.grads_t[self.index] = to_rows(refs.out_grad[self.rows, self.wide]).T
        unit, reciprocal, normed = norm(refs.k[self.rows, self.narrow], refs.key_gain)
        refs.units_k[self.index] = unit
        refs.recips_k[self.index] = jnp.broadcast_to(reciprocal, unit.shape)
        refs.own_keys[self.index] = normed.astype(BF16)

    def load(self):
        refs = self.refs
        self.queries = refs.queries[self.index]
        self.keys = jnp.concatenate(
            [refs.pool_keys[self.head, self.prompt], refs.own_keys[self.index]], axis=0
        )
        self.values = jnp.concatenate(
            [refs.pool_values[self.head, self.prompt], refs.v[self.rows, self.narrow]], axis=0
        )
        self.grads = to_rows(refs.out_grad[self.rows, self.wide])

    def scores(self):
        self.s = dot(self.queries, self.keys, 1, 1)

    def softmax(self):
        s = self.s
        own_shape = (s.shape[0], CL)
        token = lax.broadcasted_iota(jnp.int32, own_shape, 0) % CL
        column = lax.broadcasted_iota(jnp.int32, own_shape, 1)
        own = jnp.where(column <= token, s[:, PL:], -jnp.inf)
        s = jnp.concatenate([s[:, :PL], own], axis=1)
        weights = jnp.exp2((s - jnp.max(s, axis=-1, keepdims=True)) * EXPONENT)
        self.p = weights * (1.0 / jnp.sum(weights, axis=-1, keepdims=True))
        self.p_half = self.p.astype(BF16)
        self.p_rest = (self.p - self.p_half.astype(F32)).astype(BF16)

    def dp(self):
        self.dp_ = dot(self.grads, self.values, 1, 1)

    def out(self):
        refs = self.refs
        total = dot(self.p_half, self.values, 1, 0) + dot(self.p_rest, self.values, 1, 0)
        self.attended = (total * self.alive).astype(BF16)
        self.emit(refs.held_attended, refs.out_attended, 0, self.wide, to_columns(self.attended))

    def ds(self):
        delta = jnp.sum(
            self.grads.astype(F32) * self.attended.astype(F32), axis=-1, keepdims=True
        )
        self.ds_ = (self.p * (self.dp_ - delta)).astype(BF16)

    def dv(self):
        self.dv_ = dot(self.refs.grads_t[self.index], self.p_half, 1, 0)

    def dk(self):
        self.dk_ = dot(self.refs.queries_t[self.index], self.ds_, 1, 0)

    def add(self, sums, grad, scale):
        for p in range(2):
            term = grad[:, :PL] * (self.shares[p] * scale)
            if self.slot > 0:
                term += sums[self.head, p]
            sums[self.head, p] = term

    def dq(self):
        self.dq_ = dot(self.ds_, self.keys, 1, 0) * (SCALE * self.alive)

    def finish(self):
        refs = self.refs
        unit, reciprocal = refs.units_q[self.index], refs.recips_q[self.index]
        back = norm_back(self.dq_, unit, reciprocal, refs.query_gain)
        self.emit(refs.held_dq, refs.out_dq, 1, self.wide, to_columns(back.astype(BF16)))

    def own(self):
        refs = self.refs
        own = self.dk_[:, PL:].T * (SCALE * self.alive)
        terms = jnp.sum(own * self.keys[PL:].astype(F32), axis=0, keepdims=True)
        refs.gain[0:1] += terms / refs.query_gain
        refs.gain[1:2] += jnp.sum(own * refs.units_k[self.index], axis=0, keepdims=True)
        self.own_dk = own

    def finish_own(self):
        refs, own = self.refs, self.own_dk
        back = norm_back(
            own, refs.units_k[self.index], refs.recips_k[self.index], refs.key_gain
        )
        self.emit(refs.held_dk, refs.out_dk, 2, self.narrow, back.astype(BF16))
        self.emit(refs.held_dv, refs.out_dv, 3, self.narrow, (self.dv_[:, PL:].T * self.alive).astype(BF16))

    def emit(self, held, target, which, columns, block):
        held[self.rows, columns] = block
        copy = pltpu.make_async_copy(
            held.at[self.rows, columns],
            target.at[self.rows, columns],
            self.refs.out_sem.at[which, self.index],
        )
        copy.start()
        self.refs.copies.append(copy)


def unpack_pool(refs, head):
    a = refs.pool_a[:, :, head].astype(F32).reshape(16, BLOCK, HD)
    b = refs.pool_b[:, :, head].astype(F32)
    for p in range(2):
        rows = slice(24 * p, 24 * p + 24)
        refs.pool_keys[head, p] = a[:, rows].reshape(PL, HD).astype(BF16)
        refs.pool_values[head, p] = jnp.concatenate(
            [b[xx, yy, rows] for yy in range(4) for xx in range(4)], axis=0
        ).astype(BF16)


def pack_keys(refs, head):
    sums = [refs.key_sum[head, p].T for p in range(2)]
    terms = sum(sums[p] * refs.pool_keys[head, p].astype(F32) for p in range(2))
    terms = jnp.sum(terms, axis=0, keepdims=True)
    refs.gain[0:1] += terms / refs.query_gain
    refs.gain[1:2] += terms / refs.key_gain
    sums = [total.reshape(4, 4, 24, HD) for total in sums]
    refs.grad_a[head] = jnp.concatenate(sums, axis=2).astype(BF16)


def pack_values(refs, head):
    sums = [refs.value_sum[head, p].T.reshape(4, 4, 24, HD) for p in range(2)]
    for xx in range(4):
        for yy in range(4):
            refs.grad_b[head, xx, yy] = jnp.concatenate(
                [total[yy, xx] for total in sums], axis=0
            ).astype(BF16)


class Links:
    def __init__(self, refs):
        self.refs = refs
        z, y, x, tp = place()
        self.z, self.y, self.x, self.tp = z, y, x, tp
        self.here = z * 4 + tp

        def at(zz, yy, xx):
            return (zz * 16 + yy * 4 + xx, tp)

        turns = (1, 2, 3)
        self.z_peers = [at((z + d) % 4, y, x) for d in turns]
        self.y_peers = [at(z, (y + d) % 4, x) for d in turns]
        self.x_peers = [at(z, y, (x + d) % 4) for d in turns]
        self.spot = y * 4 + x
        plane = [(self.spot + d) % 16 for d in range(1, 16)]
        self.plane = [(z * 16 + spot, tp) for spot in plane]
        around = [(self.here + d) % 16 for d in range(1, 16)]
        self.around = [(other // 4 * 16 + self.spot, other % 4) for other in around]
        places = [[(z * 4 + fast + d) % 16 for d in range(1, 16)] for fast in (x, y)]
        self.others = places
        self.near = (
            [at(other // 4, y, other % 4) for other in places[0]],
            [at(other // 4, other % 4, x) for other in places[1]],
        )
        self.sent = []
        self.halves = ((y, x, self.y_peers), (x, y, self.x_peers))
        self.beside = (self.x_peers, self.y_peers)
        self.nears, self.far, self.firsts, self.lasts = {}, {}, {}, {}

    def greeted(self):
        grp = self.z * 16 + self.spot
        rest = [(grp, (self.tp + d) % 4) for d in (1, 2, 3)]
        return self.z_peers + self.y_peers + self.x_peers + rest

    def send(self, *args):
        copy = send(*args)
        self.sent.append(copy)
        return copy

    def pool(self, half):
        return self.refs.pool_b if half else self.refs.pool_a

    def prepare(self):
        refs = self.refs
        parts = [
            norm(refs.keys[:, head * HD : (head + 1) * HD], refs.key_gain)[2] for head in range(2)
        ]
        mine = jnp.concatenate(parts + [refs.values[...].astype(F32)], axis=1)
        mine = jnp.concatenate([mine, jnp.zeros((PAD - OWN, 4 * HD), F32)], axis=0)
        refs.columns[self.z] = mine.astype(BF16)

    def columns(self):
        refs = self.refs
        ref = refs.columns.at[self.z]
        self.z_copies = [
            self.send(ref, ref, refs.z_send.at[d], refs.z_recv.at[d], self.z_peers[d])
            for d in range(3)
        ]

    def block(self):
        refs = self.refs
        for copy in self.z_copies:
            copy.wait_recv()
        block = jnp.concatenate(
            [refs.columns[zz].astype(F32)[:OWN] for zz in range(4)], axis=0
        ).astype(BF16)
        for head in range(2):
            for half, (slow, fast, far) in enumerate(self.halves):
                column = (half * 2 + head) * HD
                self.pool(half)[slow, fast, head] = block[:, column : column + HD]
        for half, (slow, fast, far) in enumerate(self.halves):
            ref = self.pool(half).at[slow, fast]
            sems = refs.near_send, refs.near_recv
            self.nears[half] = [
                self.send(ref, ref, sems[0].at[half, d], sems[1].at[half, d], self.beside[half][d])
                for d in range(3)
            ]

    def forward(self, head):
        for half, (slow, fast, far) in enumerate(self.halves):
            if head == 0:
                for copy in self.nears[half]:
                    copy.wait_recv()
            ref = self.pool(half).at[slow, :, head]
            sems = self.refs.far_send, self.refs.far_recv
            self.far[head, half] = [
                self.send(ref, ref, sems[0].at[head, half, d], sems[1].at[head, half, d], far[d])
                for d in range(3)
            ]

    def arrived(self, head):
        for half in range(2):
            for copy in self.far[head, half]:
                copy.wait_recv()

    def grad(self, half):
        return self.refs.grad_b if half else self.refs.grad_a

    def first(self, head, half):
        slow, fast, far = self.halves[half]
        sems = self.refs.first_send, self.refs.first_recv
        self.firsts[head, half] = [
            self.send(
                self.grad(half).at[head, (slow + 1 + d) % 4],
                self.refs.first_in.at[head, half, d],
                sems[0].at[head, half, d],
                sems[1].at[head, half, d],
                far[d],
            )
            for d in range(3)
        ]

    def second(self, head, half):
        refs = self.refs
        slow, fast, far = self.halves[half]
        for copy in self.firsts[head, half]:
            copy.wait_recv()
        pad = jnp.zeros((PAD - OWN, HD), F32)
        for place in range(4):
            part = self.grad(half)[head, slow, place].astype(F32)
            for d in range(3):
                part += refs.first_in[head, half, d, place].astype(F32)
            for zz in range(4):
                piece = jnp.concatenate([part[zz * OWN : (zz + 1) * OWN], pad], axis=0)
                refs.own_sum[head, half, zz * 4 + place] = piece
                refs.last_out[head, half, zz * 4 + place] = piece.astype(BF16)
        self.lasts[head, half] = [
            self.send(
                refs.last_out.at[head, half, other],
                refs.last_in.at[head, half, d],
                refs.last_send.at[head, half, d],
                refs.last_recv.at[head, half, d],
                peer,
            )
            for d, (other, peer) in enumerate(zip(self.others[half], self.near[half]))
        ]

    def total(self, head, half):
        refs = self.refs
        slow, fast, far = self.halves[half]
        for copy in self.lasts[head, half]:
            copy.wait_recv()
        total = refs.own_sum[head, half, self.z * 4 + fast]
        total += jnp.sum(refs.last_in[head, half].astype(F32), axis=0)
        return total[:OWN]

    def around_gains(self):
        refs = self.refs
        refs.around_gains[self.here] = refs.gain[...]
        ref = refs.around_gains.at[self.here]
        self.gains = [
            self.send(ref, ref, refs.around_send.at[d], refs.around_recv.at[d], self.around[d])
            for d in range(15)
        ]

    def plane_gains(self):
        refs = self.refs
        for copy in self.gains:
            copy.wait_recv()
        refs.plane_gains[self.spot] = jnp.sum(refs.around_gains[...], axis=0)
        ref = refs.plane_gains.at[self.spot]
        self.gains = [
            self.send(ref, ref, refs.plane_send.at[d], refs.plane_recv.at[d], self.plane[d])
            for d in range(15)
        ]

    def total_gains(self):
        for copy in self.gains:
            copy.wait_recv()
        return jnp.sum(self.refs.plane_gains[...], axis=0)


DEFERRED = 0
PIECE = 64


def scratch_of(shapes):
    vmem, dma = pltpu.VMEM, pltpu.SemaphoreType.DMA
    wide, narrow, prompt = shapes
    return dict(
        keys=vmem(prompt, BF16),
        values=vmem(prompt, BF16),
        query_gain=vmem((1, HD), F32),
        key_gain=vmem((1, HD), F32),
        q=vmem(wide, BF16),
        k=vmem(narrow, BF16),
        v=vmem(narrow, BF16),
        out_grad=vmem(wide, BF16),
        live=pltpu.SMEM((1,), jnp.int32),
        prompts=pltpu.SMEM((4,), jnp.int32),
        in_sem=dma((10,)),
        units_q=vmem((8, HEADS * CL, HD), F32),
        recips_q=vmem((8, HEADS * CL, HD), F32),
        queries=vmem((8, HEADS * CL, HD), BF16),
        queries_t=vmem((8, HD, HEADS * CL), BF16),
        grads_t=vmem((8, HD, HEADS * CL), BF16),
        units_k=vmem((8, CL, HD), F32),
        recips_k=vmem((8, CL, HD), F32),
        own_keys=vmem((8, CL, HD), BF16),
        pool_keys=vmem((2, 2, PL, HD), BF16),
        pool_values=vmem((2, 2, PL, HD), BF16),
        key_sum=vmem((2, 2, HD, PL), F32),
        value_sum=vmem((2, 2, HD, PL), F32),
        held_attended=vmem(wide, BF16),
        held_dq=vmem(wide, BF16),
        held_dk=vmem(narrow, BF16),
        held_dv=vmem(narrow, BF16),
        held_prompt_dk=vmem(prompt, F32),
        held_prompt_dv=vmem(prompt, F32),
        out_sem=dma((4, 8)),
        late_sem=dma((4,)),
        gain=vmem((8, HD), F32),
        columns=vmem((4, PAD, 4 * HD), BF16),
        pool_a=vmem((4, 4, 2, BLOCK, HD), BF16),
        pool_b=vmem((4, 4, 2, BLOCK, HD), BF16),
        grad_a=vmem((2, 4, 4, BLOCK, HD), BF16),
        grad_b=vmem((2, 4, 4, BLOCK, HD), BF16),
        first_in=vmem((2, 2, 3, 4, BLOCK, HD), BF16),
        own_sum=vmem((2, 2, 16, PAD, HD), F32),
        last_out=vmem((2, 2, 16, PAD, HD), BF16),
        last_in=vmem((2, 2, 15, PAD, HD), BF16),
        plane_gains=vmem((16, 8, HD), F32),
        around_gains=vmem((16, 8, HD), F32),
        total_gains=vmem((8, HD), F32),
        z_send=dma((3,)),
        z_recv=dma((3,)),
        near_send=dma((2, 3)),
        near_recv=dma((2, 3)),
        far_send=dma((2, 2, 3)),
        far_recv=dma((2, 2, 3)),
        first_send=dma((2, 2, 3)),
        first_recv=dma((2, 2, 3)),
        last_send=dma((2, 2, 15)),
        last_recv=dma((2, 2, 15)),
        plane_send=dma((15,)),
        plane_recv=dma((15,)),
        around_send=dma((15,)),
        around_recv=dma((15,)),
    )


def main_kernel(names, *refs):
    refs = types.SimpleNamespace(**dict(zip(names, refs)))
    moves = (
        (refs.in_keys, refs.keys),
        (refs.in_values, refs.values),
        (refs.in_query_gain, refs.query_gain),
        (refs.in_key_gain, refs.key_gain),
        (refs.in_q, refs.q),
        (refs.in_k, refs.k),
        (refs.in_v, refs.v),
        (refs.in_out_grad, refs.out_grad),
        (refs.in_live, refs.live),
        (refs.in_prompts, refs.prompts),
    )
    entering = [
        pltpu.make_async_copy(source, target, refs.in_sem.at[i])
        for i, (source, target) in enumerate(moves)
    ]
    for copy in entering:
        copy.start()
    links = Links(refs)
    wait_for_greetings = greet(links.greeted())
    for copy in entering[:4]:
        copy.wait()
    refs.query_gain, refs.key_gain = refs.query_gain[...], refs.key_gain[...]
    links.prepare()
    wait_for_greetings()
    links.columns()
    for copy in entering[4:]:
        copy.wait()
    refs.gain[...] = jnp.zeros_like(refs.gain)
    refs.copies = []
    units = [Unit(refs, head, slot) for head in range(2) for slot in range(4)]
    for unit in units:
        unit.scalars()
    for unit in units[:4]:
        unit.prepare()
    links.block()
    links.forward(0)
    for unit in units[4:]:
        unit.prepare()
    links.forward(1)
    count = len(units)
    links.arrived(0)
    unpack_pool(refs, 0)
    units[0].load()
    units[0].scores()
    for now in range(count + 1):
        unit = units[now] if now < count else None
        before = units[now - 1] if now > 0 else None
        if now + 1 < count:
            if now == 2:
                links.arrived(1)
                unpack_pool(refs, 1)
            units[now + 1].load()
            units[now + 1].scores()
        if unit:
            unit.softmax()
            unit.dp()
        if unit:
            unit.out()
        if before:
            before.add(refs.value_sum, before.dv_, 1.0)
            if now % 4 == 0:
                pack_values(refs, before.head)
                links.first(before.head, 1)
            before.dk()
            before.add(refs.key_sum, before.dk_, SCALE)
            before.own()
            if now % 4 == 0:
                pack_keys(refs, before.head)
                links.first(before.head, 0)
        if before and now <= DEFERRED:
            before.dq()
        if unit:
            unit.ds()
            unit.dv()
        if before and now <= DEFERRED:
            before.finish()
    links.around_gains()
    for half in (1, 0):
        links.second(0, half)
    for unit in units[DEFERRED:]:
        unit.dq()
        unit.finish()
    for unit in units:
        unit.finish_own()
    for half in (1, 0):
        links.second(1, half)
    links.plane_gains()
    late = []

    def leave(source, target):
        copy = pltpu.make_async_copy(source, target, refs.late_sem.at[len(late)])
        copy.start()
        late.append(copy)

    for copy in links.sent:
        copy.wait_send()
    for copy in refs.copies:
        copy.wait()
    for head in range(2):
        columns = slice(head * HD, (head + 1) * HD)
        refs.held_prompt_dv[:, columns] = links.total(head, 1)
        unit, reciprocal, _ = norm(refs.keys[:, columns], refs.key_gain)
        refs.held_prompt_dk[:, columns] = norm_back(
            links.total(head, 0), unit, reciprocal, refs.key_gain
        )
    leave(refs.held_prompt_dv, refs.out_prompt_dv)
    leave(refs.held_prompt_dk, refs.out_prompt_dk)
    refs.total_gains[...] = links.total_gains()
    leave(refs.total_gains.at[0:1], refs.out_query_total)
    leave(refs.total_gains.at[1:2], refs.out_key_total)
    for copy in late:
        copy.wait()


def main(**arrays):
    wide, narrow, prompt = (arrays[name].shape for name in ("in_q", "in_k", "in_keys"))
    scratch = scratch_of((wide, narrow, prompt))
    hbm = pl.BlockSpec(memory_space=pltpu.HBM)
    shape = jax.ShapeDtypeStruct
    outs = dict(
        out_attended=shape(wide, BF16),
        out_dq=shape(wide, BF16),
        out_dk=shape(narrow, BF16),
        out_dv=shape(narrow, BF16),
        out_prompt_dk=shape(prompt, F32),
        out_prompt_dv=shape(prompt, F32),
        out_query_total=shape((1, HD), F32),
        out_key_total=shape((1, HD), F32),
    )
    return pl.pallas_call(
        functools.partial(main_kernel, [*arrays, *outs, *scratch]),
        out_shape=list(outs.values()),
        in_specs=[hbm] * len(arrays),
        out_specs=[hbm] * len(outs),
        scratch_shapes=list(scratch.values()),
        compiler_params=pltpu.CompilerParams(
            collective_id=0, has_side_effects=True, vmem_limit_bytes=60 << 20
        ),
    )(*arrays.values())


def copy_kernel(*refs):
    count = (len(refs) - 1) // 3
    sources, targets, held = refs[:count], refs[count : 2 * count], refs[2 * count : 3 * count]
    sem = refs[-1]
    pairs = []
    for source, target, between in zip(sources, targets, held):
        rows = source.shape[0]
        piece = min(rows, PIECE)
        for start in range(0, rows, piece):
            at, now = pl.ds(start, piece), len(pairs)
            entering = pltpu.make_async_copy(source.at[at], between.at[at], sem.at[0, now])
            leaving = pltpu.make_async_copy(between.at[at], target.at[at], sem.at[1, now])
            entering.start()
            pairs.append((entering, leaving))
    for entering, leaving in pairs:
        entering.wait()
        leaving.start()
    for entering, leaving in pairs:
        leaving.wait()


def copy_out(arrays):
    hbm = pl.BlockSpec(memory_space=pltpu.HBM)
    return pl.pallas_call(
        copy_kernel,
        out_shape=[jax.ShapeDtypeStruct(array.shape, array.dtype) for array in arrays],
        in_specs=[hbm] * len(arrays),
        out_specs=[hbm] * len(arrays),
        scratch_shapes=[pltpu.VMEM(array.shape, array.dtype) for array in arrays]
        + [pltpu.SemaphoreType.DMA((2, 32))],
        compiler_params=pltpu.CompilerParams(vmem_limit_bytes=60 << 20),
    )(*arrays)


def local(
    comp_queries,
    comp_keys,
    comp_values,
    prompt_keys,
    prompt_values,
    query_gain,
    key_gain,
    out_grad,
    live_counts,
    slot_prompts,
):
    results = main(
        in_keys=prompt_keys,
        in_values=prompt_values,
        in_query_gain=query_gain.reshape(1, HD),
        in_key_gain=key_gain.reshape(1, HD),
        in_q=comp_queries,
        in_k=comp_keys,
        in_v=comp_values,
        in_out_grad=out_grad,
        in_live=live_counts,
        in_prompts=slot_prompts,
    )
    *arrays, query_total, key_total = copy_out(results)
    return (*arrays, query_total.reshape(HD), key_total.reshape(HD))


def solution(mesh):
    both, grp = P("grp", "tp"), P("grp")
    return jax.shard_map(
        local,
        mesh=mesh,
        in_specs=(both, both, both, both, both, P(), P(), both, grp, grp),
        out_specs=(both, both, both, both, both, both, P(), P()),
        check_vma=False,
    )
```
